256 devices in a mesh: grp: 2 (over z_lo), seq: 32 (over z_hi, y, core), tp: 4 (over x).
Axes of the slice: x: 4, y: 4, z: 8 (z_hi: 4, z_lo: 2; z = z_hi * 2 + z_lo), core: 2. Of those that a mesh axis runs over, the one named last changes fastest.
Arguments:
- hidden: bfloat16 [2, 8192, 4096], P('grp', 'seq'), may hold values from -72 to 72
- w_query: bfloat16 [4096, 2048], P('seq', 'tp'), may hold values from -0.09375 to 0.09375
- w_key: bfloat16 [4096, 2048], P('seq', 'tp'), may hold values from -0.09375 to 0.09375
- w_value: bfloat16 [4096, 2048], P('seq', 'tp'), may hold values from -0.09375 to 0.09375
- prompt_len: int32 [2048], replicated, may hold values from 1 to 8192
- page_table: int32 [2048, 64], replicated, may hold values from 0 to 511, all different within a row
Outputs:
- attended: bfloat16 [2, 8192, 2048], P('grp', 'seq', 'tp')
The draws below stay inside these ranges and needn't reach their ends.
Inputs may be any that keep to these rules, and one draw needn't show every extreme that they name: `page_table`: every row lists 64 different pages; every page is listed by some row.
All inputs are finite; a program needn't handle non-finite values.
Results may differ from the reference program's by a relative error of at most 0.006.
The reference program's roundings to bfloat16 on the way count: a program that leaves them out, or rounds other values in their place, can miss the bound.
Values may be sent and summed in bfloat16 or wider, within the bound.
No kernel may reach another device: no remote copies, remote signals or barrier semaphores. Data moves between devices by JAX's collectives and lax.ppermute only.
A program may use at most 128 MiB of HBM per device.

```python
import math
import jax
import jax.numpy as jnp
from jax import lax

D = 4096
HEADS = 16
HD = 128
PAGE = 16
STEPS = 4
ROWS = 2048
PROMPT = 8192
PAGES = 512
CTXP = 64


def draw_hidden(key, part):
    base = jnp.clip(jax.random.normal(key, (2, PROMPT, D), jnp.float32), -6.0, 6.0)
    return base.astype(jnp.bfloat16)


def place_ends(values, stream_key, smallest, largest):
    longest = values.shape.index(max(values.shape))
    spots = []
    for shift in (0, 1):
        where = [jax.random.randint(jax.random.fold_in(stream_key, axis), (), 0, length) for axis, length in enumerate(values.shape)]
        where[longest] = (where[longest] + shift) % values.shape[longest]
        spots.append(tuple(where))
    return values.at[spots[0]].set(smallest).at[spots[1]].set(largest)


def block_levels(key, shape, cuts, least, high):
    factor_of = 1.0
    for dim, blocks in cuts:
        draws = jax.random.uniform(jax.random.fold_in(jax.random.fold_in(key, 6), dim), (blocks,), jnp.float32, least / len(cuts), high / len(cuts))
        factor_of = factor_of * jnp.repeat(jnp.exp(draws), shape[dim] // blocks).reshape((-1,) + (1,) * (len(shape) - 1 - dim))
    return factor_of


def different_ones(key, rows, amount, top, lift):
    ranking = jax.random.permutation(jax.random.fold_in(key, 1), amount)
    boost = ranking
    for power in range(3):
        boost = boost * boost // amount
    boost = boost * lift // amount
    chance = jax.random.randint(jax.random.fold_in(key, 2), (rows, amount), 0, 4096) + boost
    sure = jax.random.permutation(jax.random.fold_in(key, 3), rows)[jnp.arange(amount) % rows]
    chance = jnp.where(jnp.arange(rows)[:, None] == sure[None, :], 1 << 14, chance)
    score = chance * amount + jnp.arange(amount)
    return lax.top_k(score.astype(jnp.int32), top)[1].astype(jnp.int32)


def gaussian(stream_key, shape, deviation, reach, cuts=(), kind=jnp.bfloat16):
    loudness = block_levels(stream_key, shape, cuts, -0.22, 0.18) if cuts else 1.0
    values = jax.random.normal(stream_key, shape, jnp.float32) * deviation * loudness
    return jnp.minimum(jnp.maximum(values, -reach), reach).astype(kind)


def setup_inputs(seed: int = 0) -> dict:
    key_of = jax.random.split(jax.random.key(seed), 7)
    hidden = draw_hidden(jax.random.fold_in(key_of[6], 71), 0)
    w_query = gaussian(key_of[1], (D, HEADS * HD), D ** -0.5, 0.09375, ((0, 32), (1, 4)))
    w_key = gaussian(key_of[2], (D, HEADS * HD), D ** -0.5, 0.09375, ((0, 32), (1, 4)))
    w_value = gaussian(key_of[3], (D, HEADS * HD), D ** -0.5, 0.09375, ((0, 32), (1, 4)))
    prompt_len = place_ends(jax.random.randint(key_of[4], (ROWS,), 1, PROMPT + 1), jax.random.fold_in(key_of[4], 1), 1, PROMPT).astype(jnp.int32)
    page_table = different_ones(key_of[5], ROWS, PAGES, CTXP, 1024)
    return {"hidden": hidden, "w_query": w_query, "w_key": w_key, "w_value": w_value, "prompt_len": prompt_len, "page_table": page_table}


NEG = -1.0e30


def attend_head(query, keys, values, allowed):
    scores = jnp.dot(query, keys.T, preferred_element_type=jnp.float32) * (HD ** -0.5)
    scores = jnp.where(allowed, scores, NEG)
    top = jnp.max(scores, axis=1, keepdims=True)
    weights = jnp.where(allowed, jnp.exp(scores - top), 0.0)
    total = jnp.sum(weights, axis=1, keepdims=True)
    summed = jnp.dot(weights.astype(jnp.bfloat16), values, preferred_element_type=jnp.float32)
    return summed / total


def reference(hidden, w_query, w_key, w_value, prompt_len, page_table):
    flat_hidden = hidden.reshape(2 * PROMPT, D)

    def project(weight):
        out = jnp.dot(flat_hidden, weight, preferred_element_type=jnp.float32).astype(jnp.bfloat16)
        return out.reshape(2, PROMPT, HEADS, HD)

    query, keys, values = project(w_query), project(w_key), project(w_value)
    qblock = math.gcd(PROMPT, 512)

    def prefill_head(head):
        head_query, head_keys, head_values = head
        pieces = []
        for index in range(PROMPT // qblock):
            begin = index * qblock
            end = begin + qblock
            query_pos = jnp.arange(begin, end).astype(jnp.int32)
            key_pos = jnp.arange(end).astype(jnp.int32)
            allowed = key_pos[None, :] <= query_pos[:, None]
            pieces.append(attend_head(head_query[begin:end], head_keys[:end], head_values[:end], allowed))
        return jnp.concatenate(pieces, axis=0).astype(jnp.bfloat16)

    prefill = lax.map(prefill_head, (query[0].transpose(1, 0, 2), keys[0].transpose(1, 0, 2), values[0].transpose(1, 0, 2)))
    prefill = prefill.transpose(1, 0, 2).reshape(PROMPT, HEADS * HD)

    rblock = math.gcd(ROWS, 8)
    offsets = jnp.arange(PAGE).astype(jnp.int32)
    causal_steps = jnp.arange(STEPS)[None, :] <= jnp.arange(STEPS)[:, None]

    def decode_block(index):
        first_row = index * rblock
        tables = lax.dynamic_slice_in_dim(page_table, first_row, rblock, 0)
        lengths = lax.dynamic_slice_in_dim(prompt_len, first_row, rblock, 0)
        key_pos = (tables[:, :, None] * PAGE + offsets[None, None, :]).reshape(rblock, CTXP * PAGE)
        context_allowed = key_pos < lengths[:, None]
        context_keys = keys[0][key_pos]
        context_values = values[0][key_pos]
        first_pos = first_row * STEPS
        block_query = lax.dynamic_slice_in_dim(query[1], first_pos, rblock * STEPS, 0).reshape(rblock, STEPS, HEADS, HD)
        own_keys = lax.dynamic_slice_in_dim(keys[1], first_pos, rblock * STEPS, 0).reshape(rblock, STEPS, HEADS, HD)
        own_values = lax.dynamic_slice_in_dim(values[1], first_pos, rblock * STEPS, 0).reshape(rblock, STEPS, HEADS, HD)
        all_keys = jnp.concatenate([context_keys, own_keys], axis=1)
        all_values = jnp.concatenate([context_values, own_values], axis=1)
        allowed = jnp.concatenate([
            jnp.broadcast_to(context_allowed[:, None, :], (rblock, STEPS, CTXP * PAGE)),
            jnp.broadcast_to(causal_steps[None], (rblock, STEPS, STEPS))], axis=2)
        scores = jnp.einsum("rshd,rkhd->rhsk", block_query.astype(jnp.float32), all_keys.astype(jnp.float32)) * (HD ** -0.5)
        scores = jnp.where(allowed[:, None], scores, NEG)
        top = jnp.max(scores, axis=3, keepdims=True)
        weights = jnp.where(allowed[:, None], jnp.exp(scores - top), 0.0)
        total = jnp.sum(weights, axis=3)
        summed = jnp.einsum("rhsk,rkhd->rshd", weights.astype(jnp.bfloat16).astype(jnp.float32), all_values.astype(jnp.float32))
        result = summed / total.transpose(0, 2, 1)[:, :, :, None]
        return result.reshape(rblock * STEPS, HEADS * HD).astype(jnp.bfloat16)

    decode = lax.map(decode_block, jnp.arange(ROWS // rblock).astype(jnp.int32)).reshape(PROMPT, HEADS * HD)
    return jnp.stack([prefill, decode])
```

```python
import jax
import jax.numpy as jnp
from jax import lax
from jax.experimental import pallas as pl
from jax.experimental.pallas import tpu as pltpu
from jax.sharding import Mesh, PartitionSpec as P

HD = 128
PAGE = 16
STEPS = 4
NEG = -1e30
SCALE = HD ** -0.5 * 1.4426950408889634
SIZES = {"g": 2, "z": 4, "y": 4, "c": 2, "x": 4}
PART_A = 384
PART_B = 128
CHUNK = 512
TILE = 256
VMEM_LIMIT = 48 * 1024 * 1024


def shift(value, axis, by):
    count = SIZES[axis]
    return lax.ppermute(value, axis, [((k + by) % count, k) for k in range(count)])


def ring(value, axis):
    return [value, shift(value, axis, 1), shift(value, axis, 2), shift(value, axis, 3)]


def gather_two(part_a, part_b):
    first_a = jnp.concatenate(ring(part_a, "z"), axis=0)
    first_b = jnp.concatenate(ring(part_b, "y"), axis=0)
    return ring(first_a, "y"), ring(first_b, "z")


def project_kernel(table, h0, h1, h2, h3, a0, a1, a2, a3, b0, b1, b2, b3, kv_out, q_out, w_kv, w_q):
    for i, (a, b) in enumerate(zip((a0, a1, a2, a3), (b0, b1, b2, b3))):
        for j in range(4):
            rows = pl.ds(j * 256, 256)
            w_kv[pl.ds(pl.multiple_of(table[4 * i + j] * 256, 256), 256), :] = a[rows, :]
            w_q[pl.ds(pl.multiple_of(table[16 + 4 * i + j] * 256, 256), 256), :] = b[rows, :]
    for k, h in enumerate((h0, h1, h2, h3)):
        rows = pl.ds(pl.multiple_of(table[32 + k] * 256, 256), 256)
        kv_out[rows, :] = jnp.dot(h[...], w_kv[...], preferred_element_type=jnp.float32).astype(jnp.bfloat16)
        q_out[rows, :] = jnp.dot(h[...], w_q[...], preferred_element_type=jnp.float32).astype(jnp.bfloat16)


def project(table, hiddens, parts_a, parts_b):
    vmem = pl.BlockSpec(memory_space=pltpu.VMEM)
    return pl.pallas_call(
        project_kernel,
        out_shape=(
            jax.ShapeDtypeStruct((2 * CHUNK, 2 * HD), jnp.bfloat16),
            jax.ShapeDtypeStruct((2 * CHUNK, HD), jnp.bfloat16),
        ),
        in_specs=[pl.BlockSpec(memory_space=pltpu.SMEM)] + [vmem] * 12,
        out_specs=(vmem, vmem),
        scratch_shapes=[
            pltpu.VMEM((4096, 2 * HD), jnp.bfloat16),
            pltpu.VMEM((4096, HD), jnp.bfloat16),
        ],
        compiler_params=pltpu.CompilerParams(vmem_limit_bytes=VMEM_LIMIT),
        cost_estimate=pl.CostEstimate(
            flops=2 * 1024 * 4096 * 384, bytes_accessed=12 * 1024 * 1024, transcendentals=0
        ),
        name="project",
    )(table, *hiddens, *parts_a, *parts_b)


def scores_of(query, keys):
    return lax.dot_general(query, keys, (((1,), (1,)), ((), ())), preferred_element_type=jnp.float32)


def attend_kernel(
    q_ref, own_ref, bias_ref, pos_ref, len_ref, a0, a1, a2, a3, b0, b1, b2, b3, out_ref, keys, vals, top, acc
):
    block = 4 * CHUNK
    row_page = lax.broadcasted_iota(jnp.int32, (block, HD), 0) // PAGE
    column = lax.broadcasted_iota(jnp.int32, (block, HD), 1)
    keys[:, HD:] = jnp.where(row_page == column, 1.0, 0.0).astype(jnp.bfloat16)
    vals[:, HD:] = jnp.ones((block, HD), jnp.bfloat16)

    for tile in range(4):
        rows = pl.ds(tile * TILE, TILE)
        first = 0 if tile < 2 else tile * TILE
        count = (tile + 1) * TILE - first
        query_pos = tile * TILE - first + lax.broadcasted_iota(jnp.int32, (TILE, count), 0)
        key_pos = lax.broadcasted_iota(jnp.int32, (TILE, count), 1)
        allowed = key_pos <= query_pos
        if tile >= 2:
            allowed &= (key_pos // STEPS) == (query_pos // STEPS)
        scores = scores_of(q_ref[rows, :], own_ref[pl.ds(first, count), :HD])
        scores = jnp.where(allowed, scores, NEG)
        best = jnp.max(scores, axis=1, keepdims=True)
        weights = jnp.exp2((scores - best) * SCALE).astype(jnp.bfloat16)
        own_vals = jnp.concatenate(
            [own_ref[pl.ds(first, count), HD:], jnp.ones((count, HD), jnp.bfloat16)], axis=1
        )
        acc[rows, :] = jnp.dot(weights, own_vals, preferred_element_type=jnp.float32)
        top[rows, :] = jnp.broadcast_to(best, (TILE, HD))

    for i, (a, b) in enumerate(zip((a0, a1, a2, a3), (b0, b1, b2, b3))):
        split = 4 * PART_A
        keys[:split, :HD] = a[:, :HD]
        keys[split:, :HD] = b[:, :HD]
        vals[:split, :HD] = a[:, HD:]
        vals[split:, :HD] = b[:, HD:]

        def one_tile(tile, decode):
            rows = pl.ds(pl.multiple_of(tile * TILE, TILE), TILE)
            query = jnp.concatenate([q_ref[rows, :], bias_ref[rows, i * HD:(i + 1) * HD]], axis=1)
            scores = scores_of(query, keys[...])
            if decode:
                length = len_ref[pl.ds(pl.multiple_of((tile - 2) * TILE, TILE), TILE), :]
                scores = jnp.where(pos_ref[:, i * block:(i + 1) * block] < length, scores, NEG)
            before = top[rows, :1]
            best = jnp.maximum(before, jnp.max(scores, axis=1, keepdims=True))
            weights = jnp.exp2((scores - best) * SCALE).astype(jnp.bfloat16)
            summed = jnp.dot(weights, vals[...], preferred_element_type=jnp.float32)
            acc[rows, :] = acc[rows, :] * jnp.exp2((before - best) * SCALE) + summed
            top[rows, :] = jnp.broadcast_to(best, (TILE, HD))

        @pl.loop(0, 2)
        def prompt_tiles(tile):
            one_tile(tile, False)

        @pl.loop(2, 4)
        def decode_tiles(tile):
            one_tile(tile, True)

    out_ref[...] = (acc[:, :HD] / acc[:, HD:]).astype(jnp.bfloat16)


def attend(query, own, bias, pos, lengths, parts_a, parts_b):
    vmem = pl.BlockSpec(memory_space=pltpu.VMEM)
    return pl.pallas_call(
        attend_kernel,
        out_shape=jax.ShapeDtypeStruct((2 * CHUNK, HD), jnp.bfloat16),
        in_specs=[vmem] * 13,
        out_specs=vmem,
        scratch_shapes=[
            pltpu.VMEM((4 * CHUNK, 2 * HD), jnp.bfloat16),
            pltpu.VMEM((4 * CHUNK, 2 * HD), jnp.bfloat16),
            pltpu.VMEM((2 * CHUNK, HD), jnp.float32),
            pltpu.VMEM((2 * CHUNK, 2 * HD), jnp.float32),
        ],
        compiler_params=pltpu.CompilerParams(vmem_limit_bytes=VMEM_LIMIT),
        cost_estimate=pl.CostEstimate(
            flops=4 * 1024 * 8192 * 256, bytes_accessed=6 * 1024 * 1024, transcendentals=1024 * 8192
        ),
        name="attend",
    )(query, own, bias, pos, lengths, *parts_a, *parts_b)


def on_device(hidden, w_query, w_key, w_value, prompt_len, page_table):
    g, z, y, c, x = (lax.axis_index(name) for name in ("g", "z", "y", "c", "x"))
    local = hidden[0]

    with jax.named_scope("weights"):
        def head_of(head):
            pieces = [lax.dynamic_slice_in_dim(w, head * HD, HD, 1) for w in (w_key, w_value, w_query)]
            return jnp.concatenate(pieces, axis=1)

        mine = head_of(2 * g + c)
        other = shift(head_of(2 * g + 1 - c), "c", 1)
        both = jnp.where(c == 0, jnp.concatenate([mine, other]), jnp.concatenate([other, mine]))
        weights_a, weights_b = gather_two(both[:, :2 * HD], both[:, 2 * HD:])

    with jax.named_scope("hidden"):
        local_other = shift(local, "c", 1)
        quarter = shift(lax.dynamic_slice_in_dim(local, x * 64, 64, 0), "g", 1)
        remote = jnp.zeros_like(local)
        for k, piece in enumerate(ring(quarter, "x")):
            remote = lax.dynamic_update_slice_in_dim(remote, piece, ((x + k) % 4) * 64, 0)
        remote_other = shift(remote, "c", 1)

    with jax.named_scope("tables"):
        i = jnp.arange(4)[:, None]
        j = jnp.arange(4)[None, :]
        chip_a = ((z + j) % 4) * 4 + (y + i) % 4
        chip_b = ((z + i) % 4) * 4 + (y + j) % 4
        places = jnp.stack([2 * g + c, 2 * g + 1 - c, 2 * (1 - g) + c, 2 * (1 - g) + 1 - c])
        table = jnp.concatenate([chip_a.reshape(-1), chip_b.reshape(-1), places]).astype(jnp.int32)
        per_chunk = CHUNK // PAGE
        pages_a = chip_a[:, :, None] * per_chunk + jnp.arange(PART_A // PAGE)
        pages_b = chip_b[:, :, None] * per_chunk + PART_A // PAGE + jnp.arange(PART_B // PAGE)
        pages = jnp.concatenate([pages_a.reshape(4, -1), pages_b.reshape(4, -1)], axis=1).reshape(-1)
        pos = (pages[:, None] * PAGE + jnp.arange(PAGE)[None, :]).reshape(1, -1).astype(jnp.int32)
        chip = z * 4 + y
        row_count = CHUNK // STEPS
        own_table = lax.dynamic_slice_in_dim(page_table, chip * row_count, row_count, 0)
        own_len = lax.dynamic_slice_in_dim(prompt_len, chip * row_count, row_count, 0)
        listed = jnp.any(own_table[:, :, None] == pages[None, None, :], axis=1)
        listed &= pages[None, :] * PAGE < own_len[:, None]
        listed = jnp.repeat(listed, STEPS, axis=0)
        lengths = jnp.repeat(own_len, STEPS)[:, None]
        earlier = jnp.broadcast_to((pages // per_chunk < chip)[None, :], listed.shape)
        bias = jnp.where(jnp.concatenate([earlier, listed]), 0.0, NEG).astype(jnp.bfloat16)

    own, query = project(table, (local, local_other, remote, remote_other), weights_a, weights_b)
    with jax.named_scope("cache"):
        cache_a, cache_b = gather_two(own[:PART_A], own[PART_A:CHUNK])
    out = attend(query, own, bias, pos, lengths, cache_a, cache_b)

    with jax.named_scope("output"):
        tiles = out.reshape(2, 2, TILE, HD)
        kept = lax.dynamic_index_in_dim(tiles, c, 1, False)
        swapped = shift(lax.dynamic_index_in_dim(tiles, 1 - c, 1, False), "c", 1)
        pair = jnp.where(c == 0, jnp.concatenate([kept, swapped], 2), jnp.concatenate([swapped, kept], 2))
        stay = lax.dynamic_index_in_dim(pair, g, 0, False)
        come = shift(lax.dynamic_index_in_dim(pair, 1 - g, 0, False), "g", 1)
        result = jnp.where(g == 0, jnp.concatenate([stay, come], 1), jnp.concatenate([come, stay], 1))
    return result[None]


def solution(mesh):
    names = ("g", "z", "y", "c", "x")
    split = Mesh(mesh.devices.reshape([SIZES[name] for name in names]), names)
    weight = P(("z", "y", "c"), "x")
    return jax.shard_map(
        on_device,
        mesh=split,
        in_specs=(P("g", ("z", "y", "c"), None), weight, weight, weight, P(), P()),
        out_specs=P("g", ("z", "y", "c"), "x"),
        check_vma=False,
    )
```

```python
import functools

import jax
import jax.numpy as jnp
from jax import lax
from jax.experimental import pallas as pl
from jax.experimental.pallas import tpu as pltpu
from jax.sharding import Mesh, PartitionSpec as P

HD = 128
PAGE = 16
STEPS = 4
NEG = -1e30
SCALE = HD ** -0.5 * 1.4426950408889634
SIZES = {"g": 2, "z": 4, "y": 4, "c": 2, "x": 4}
CHUNK = 512
PART_A = 448
PART_B = CHUNK - PART_A
TILE = 256
ROWS = 2 * CHUNK
MIB = 1024 * 1024
VMEM = pl.BlockSpec(memory_space=pltpu.VMEM)


def shift(value, axis, by):
    count = SIZES[axis]
    return lax.ppermute(value, axis, [((k + by) % count, k) for k in range(count)])


def ring(value, axis):
    return [value, shift(value, axis, 1), shift(value, axis, 2), shift(value, axis, 3)]


def gather_a(part):
    return ring(jnp.concatenate(ring(part, "z"), axis=0), "y")


def after(value, other):
    return lax.optimization_barrier((value, other))


def project_kv_kernel(table, h0, h1, h2, a0, a1, a2, a3, kv_out, w_kv):
    for i, a in enumerate((a0, a1, a2, a3)):
        for j in range(4):
            w_kv[pl.ds(pl.multiple_of(table[4 * i + j] * 256, 256), 256), :] = a[pl.ds(j * 256, 256), :]
    for k, h in enumerate((h0, h1, h2)):
        rows = pl.ds(pl.multiple_of(table[16 + k] * 256, 256), h.shape[0])
        kv_out[rows, :] = jnp.dot(h[...], w_kv[...], preferred_element_type=jnp.float32).astype(jnp.bfloat16)


def project_kv(table, hiddens, parts):
    return pl.pallas_call(
        project_kv_kernel,
        out_shape=jax.ShapeDtypeStruct((ROWS, 2 * HD), jnp.bfloat16),
        in_specs=[pl.BlockSpec(memory_space=pltpu.SMEM)] + [VMEM] * 7,
        out_specs=VMEM,
        scratch_shapes=[pltpu.VMEM((4096, 2 * HD), jnp.bfloat16)],
        compiler_params=pltpu.CompilerParams(vmem_limit_bytes=12 * MIB),
        cost_estimate=pl.CostEstimate(
            flops=2 * ROWS * 4096 * 256, bytes_accessed=11 * MIB, transcendentals=0
        ),
        name="project_kv",
    )(table, *hiddens, *parts)


def project_q_kernel(table, h0, h1, h2, w_q, q_out):
    for k, h in enumerate((h0, h1, h2)):
        rows = pl.ds(pl.multiple_of(table[16 + k] * 256, 256), h.shape[0])
        q_out[rows, :] = jnp.dot(h[...], w_q[...], preferred_element_type=jnp.float32).astype(jnp.bfloat16)


def project_q(table, hiddens, weights):
    return pl.pallas_call(
        project_q_kernel,
        out_shape=jax.ShapeDtypeStruct((ROWS, HD), jnp.bfloat16),
        in_specs=[pl.BlockSpec(memory_space=pltpu.SMEM)] + [VMEM] * 4,
        out_specs=VMEM,
        compiler_params=pltpu.CompilerParams(vmem_limit_bytes=8 * MIB),
        cost_estimate=pl.CostEstimate(
            flops=2 * ROWS * 4096 * 256, bytes_accessed=10 * MIB, transcendentals=0
        ),
        name="project_q",
    )(table, *hiddens, weights)


def scores_of(query, keys):
    return lax.dot_general(query, keys, (((1,), (1,)), ((), ())), preferred_element_type=jnp.float32)


def attend_own_kernel(q_ref, own_ref, top, acc):
    for tile in range(4):
        rows = pl.ds(tile * TILE, TILE)
        first = 0 if tile < 2 else tile * TILE
        count = (tile + 1) * TILE - first
        query_pos = tile * TILE - first + lax.broadcasted_iota(jnp.int32, (TILE, count), 0)
        key_pos = lax.broadcasted_iota(jnp.int32, (TILE, count), 1)
        allowed = key_pos <= query_pos
        if tile >= 2:
            allowed &= (key_pos >> 2) == (query_pos >> 2)
        scores = scores_of(q_ref[rows, :], own_ref[pl.ds(first, count), :HD])
        scores = jnp.where(allowed, scores, NEG)
        best = jnp.max(scores, axis=1, keepdims=True)
        weights = jnp.exp2((scores - best) * SCALE).astype(jnp.bfloat16)
        own_vals = jnp.concatenate(
            [own_ref[pl.ds(first, count), HD:], jnp.ones((count, HD), jnp.bfloat16)], axis=1
        )
        acc[rows, :] = jnp.dot(weights, own_vals, preferred_element_type=jnp.float32)
        top[rows, :] = jnp.broadcast_to(best, (TILE, HD))


STATE = (
    jax.ShapeDtypeStruct((ROWS, HD), jnp.float32),
    jax.ShapeDtypeStruct((ROWS, 2 * HD), jnp.float32),
)


def attend_own(query, own):
    return pl.pallas_call(
        attend_own_kernel,
        out_shape=STATE,
        in_specs=[VMEM] * 2,
        out_specs=(VMEM, VMEM),
        compiler_params=pltpu.CompilerParams(vmem_limit_bytes=8 * MIB),
        cost_estimate=pl.CostEstimate(
            flops=4 * ROWS * 512 * 256, bytes_accessed=2 * MIB, transcendentals=ROWS * 384
        ),
        name="attend_own",
    )(query, own)


def attend_block_kernel(last, q_ref, bias_ref, pos_ref, len_ref, kv_ref, top_in, acc_in, *rest):
    if last:
        out_ref, keys, vals = rest
    else:
        top_out, acc_out, keys, vals = rest
    block = kv_ref.shape[0]
    row_page = lax.broadcasted_iota(jnp.int32, (block, HD), 0) >> 4
    column = lax.broadcasted_iota(jnp.int32, (block, HD), 1)
    keys[:, :HD] = kv_ref[:, :HD]
    keys[:, HD:] = jnp.where(row_page == column, 1.0, 0.0).astype(jnp.bfloat16)
    vals[:, :HD] = kv_ref[:, HD:]
    vals[:, HD:] = jnp.ones((block, HD), jnp.bfloat16)

    for tile in range(4):
        rows = pl.ds(tile * TILE, TILE)
        query = jnp.concatenate([q_ref[rows, :], bias_ref[rows, :]], axis=1)
        scores = scores_of(query, keys[...])
        if tile >= 2:
            length = len_ref[pl.ds((tile - 2) * TILE, TILE), :]
            scores = jnp.where(pos_ref[...] < length, scores, NEG)
        before = top_in[rows, :1]
        best = jnp.maximum(before, jnp.max(scores, axis=1, keepdims=True))
        weights = jnp.exp2((scores - best) * SCALE).astype(jnp.bfloat16)
        summed = jnp.dot(weights, vals[...], preferred_element_type=jnp.float32)
        state = acc_in[rows, :] * jnp.exp2((before - best) * SCALE) + summed
        if last:
            out_ref[rows, :] = (state[:, :HD] / state[:, HD:]).astype(jnp.bfloat16)
        else:
            acc_out[rows, :] = state
            top_out[rows, :] = jnp.broadcast_to(best, (TILE, HD))


def attend_block(state, query, bias, pos, lengths, block, last=False):
    count = block.shape[0]
    return pl.pallas_call(
        functools.partial(attend_block_kernel, last),
        out_shape=jax.ShapeDtypeStruct((ROWS, HD), jnp.bfloat16) if last else STATE,
        in_specs=[VMEM] * 7,
        out_specs=VMEM if last else (VMEM, VMEM),
        scratch_shapes=[pltpu.VMEM((count, 2 * HD), jnp.bfloat16)] * 2,
        compiler_params=pltpu.CompilerParams(vmem_limit_bytes=20 * MIB),
        cost_estimate=pl.CostEstimate(
            flops=4 * ROWS * count * 256, bytes_accessed=4 * MIB, transcendentals=ROWS * count
        ),
        name="attend_last" if last else "attend_block",
    )(query, bias, pos, lengths, block, *state)


def on_device(hidden, w_query, w_key, w_value, prompt_len, page_table):
    g, z, y, c, x = (lax.axis_index(name) for name in ("g", "z", "y", "c", "x"))
    local = hidden[0]

    with jax.named_scope("weights"):
        def head_of(head):
            pieces = [lax.dynamic_slice_in_dim(w, head * HD, HD, 1) for w in (w_key, w_value, w_query)]
            return jnp.concatenate(pieces, axis=1)

        mine = head_of(2 * g + c)
        other = shift(head_of(2 * g + 1 - c), "c", 1)
        both = jnp.where(c == 0, jnp.concatenate([mine, other]), jnp.concatenate([other, mine]))
        quarter = shift(lax.dynamic_slice_in_dim(local, x * 64, 64, 0), "g", 1)
        first = ring(both[:, :2 * HD], "z")
        (quarter, own_q), first = after((quarter, both[:, 2 * HD:]), first)
        weights_kv = ring(jnp.concatenate(first, axis=0), "y")

    with jax.named_scope("hidden"):
        remote = lax.all_gather(quarter, ("c", "x"), axis=0, tiled=True)
        weights_q = lax.all_gather(own_q, ("z", "y"), axis=0, tiled=True)
        hiddens = (local, shift(local, "c", 1), remote)

    with jax.named_scope("tables"):
        i = jnp.arange(4)[:, None]
        j = jnp.arange(4)[None, :]
        chip_a = ((z + j) % 4) * 4 + (y + i) % 4
        places = jnp.stack([2 * g + c, 2 * g + 1 - c, 2 * (1 - g)])
        table = jnp.concatenate([chip_a.reshape(-1), places]).astype(jnp.int32)
        per_chunk = CHUNK // PAGE
        pages_a = (chip_a[:, :, None] * per_chunk + jnp.arange(PART_A // PAGE)).reshape(4, -1)
        pad = jnp.full((4, HD - pages_a.shape[1]), -1, jnp.int32)
        pages_b = (jnp.arange(16)[:, None] * per_chunk + PART_A // PAGE + jnp.arange(PART_B // PAGE)).reshape(-1)
        pages = jnp.concatenate([
            jnp.concatenate([pages_a, pad], axis=1).reshape(-1), pages_b, jnp.full((HD - pages_b.size,), -1, jnp.int32)
        ]).astype(jnp.int32)
        pos = (pages[:, None] * PAGE + jnp.arange(PAGE)[None, :]).reshape(5, 1, HD * PAGE).astype(jnp.int32)
        chip = z * 4 + y
        row_count = CHUNK // STEPS
        own_table = lax.dynamic_slice_in_dim(page_table, chip * row_count, row_count, 0)
        own_len = lax.dynamic_slice_in_dim(prompt_len, chip * row_count, row_count, 0)
        listed = jnp.any(own_table[:, :, None] == pages[None, None, :], axis=1)
        listed &= pages[None, :] * PAGE < own_len[:, None]
        listed = jnp.repeat(listed, STEPS, axis=0)
        lengths = jnp.repeat(own_len, STEPS)[:, None]
        earlier = jnp.broadcast_to((pages // per_chunk < chip)[None, :], listed.shape)
        bias = jnp.where(jnp.concatenate([earlier, listed]), 0.0, NEG).astype(jnp.bfloat16)

    own = project_kv(table, hiddens, weights_kv)
    with jax.named_scope("cache"):
        cache_a = gather_a(own[:PART_A])
        cache_b = lax.all_gather(own[PART_A:CHUNK], ("z", "y"), axis=0, tiled=True)
    query = project_q(table, hiddens, weights_q)
    state = attend_own(query, own)
    for k in (0, 1, 3, 2):
        state = attend_block(
            state, query, bias[:, k * HD:(k + 1) * HD], pos[k, :, :4 * PART_A], lengths, cache_a[k]
        )
    out = attend_block(
        state, query, bias[:, 4 * HD:], pos[4, :, :16 * PART_B], lengths, cache_b, last=True
    )

    with jax.named_scope("output"):
        tiles = out.reshape(2, 2, TILE, HD)
        kept = lax.dynamic_index_in_dim(tiles, c, 1, False)
        swapped = shift(lax.dynamic_index_in_dim(tiles, 1 - c, 1, False), "c", 1)
        pair = jnp.where(c == 0, jnp.concatenate([kept, swapped], 2), jnp.concatenate([swapped, kept], 2))
        stay = lax.dynamic_index_in_dim(pair, g, 0, False)
        come = shift(lax.dynamic_index_in_dim(pair, 1 - g, 0, False), "g", 1)
        result = jnp.where(g == 0, jnp.concatenate([stay, come], 1), jnp.concatenate([come, stay], 1))
    return result[None]


def solution(mesh):
    names = ("g", "z", "y", "c", "x")
    split = Mesh(mesh.devices.reshape([SIZES[name] for name in names]), names)
    weight = P(("z", "y", "c"), "x")
    return jax.shard_map(
        on_device,
        mesh=split,
        in_specs=(P("g", ("z", "y", "c"), None), weight, weight, weight, P(), P()),
        out_specs=P("g", ("z", "y", "c"), "x"),
        check_vma=False,
    )
```

```python
import functools

import jax
import jax.numpy as jnp
from jax import lax
from jax.experimental import pallas as pl
from jax.experimental.pallas import tpu as pltpu
from jax.sharding import Mesh, PartitionSpec as P

HD = 128
PAGE = 16
STEPS = 4
NEG = -1e30
SCALE = HD ** -0.5 * 1.4426950408889634
SIZES = {"g": 2, "z": 4, "y": 4, "c": 2, "x": 4}
CHUNK = 512
TILE = 256
ROWS = 2 * CHUNK
MIB = 1024 * 1024
VMEM = pl.BlockSpec(memory_space=pltpu.VMEM)


def shift(value, axis, by):
    count = SIZES[axis]
    return lax.ppermute(value, axis, [((k + by) % count, k) for k in range(count)])


def ring(value, axis):
    return [value, shift(value, axis, 1), shift(value, axis, 2), shift(value, axis, 3)]


def ring_halves(value, axis):
    half = value.shape[0] // 2
    near, back = shift(value, axis, 1), shift(value, axis, 3)
    return [value, near, shift(near[:half], axis, 1), shift(back[half:], axis, 3), back]


def after(value, other):
    return lax.optimization_barrier((value, other))


def project_kernel(table, *refs):
    pieces, hiddens = refs[:9], refs[9:12]
    kv_out, q_out, w_all, h_all, sems = refs[12:]
    copies = []

    def copy(source, target):
        copies.append(pltpu.make_async_copy(source, target, sems.at[len(copies)]))
        copies[-1].start()

    place = 0
    for piece in pieces:
        for start in range(0, piece.shape[0], 128):
            rows = pl.ds(pl.multiple_of(table[place] * 128, 128), 128)
            copy(piece.at[pl.ds(start, 128), :], w_all.at[rows, :])
            place += 1
    for k, h in enumerate(hiddens):
        copy(h, h_all.at[pl.ds(k * 256, h.shape[0]), :])
    for item in copies[:-3]:
        item.wait()
    for k, h in enumerate(hiddens):
        copies[k - 3].wait()
        rows = pl.ds(pl.multiple_of(table[32 + k] * 256, 256), h.shape[0])
        result = jnp.dot(
            h_all[pl.ds(k * 256, h.shape[0]), :], w_all[...], preferred_element_type=jnp.float32
        ).astype(jnp.bfloat16)
        kv_out[rows, :] = result[:, :2 * HD]
        q_out[rows, :] = result[:, 2 * HD:]


def project(table, hiddens, parts):
    anywhere = pl.BlockSpec(memory_space=pl.ANY)
    return pl.pallas_call(
        project_kernel,
        out_shape=(
            jax.ShapeDtypeStruct((ROWS, 2 * HD), jnp.bfloat16),
            jax.ShapeDtypeStruct((ROWS, HD), jnp.bfloat16),
        ),
        in_specs=[pl.BlockSpec(memory_space=pltpu.SMEM)] + [anywhere] * 12,
        out_specs=(VMEM, VMEM),
        scratch_shapes=[
            pltpu.VMEM((4096, 3 * HD), jnp.bfloat16),
            pltpu.VMEM((ROWS, 4096), jnp.bfloat16),
            pltpu.SemaphoreType.DMA((35,)),
        ],
        compiler_params=pltpu.CompilerParams(vmem_limit_bytes=22 * MIB),
        cost_estimate=pl.CostEstimate(
            flops=2 * ROWS * 4096 * 384, bytes_accessed=12 * MIB, transcendentals=0
        ),
        name="project",
    )(table, *parts, *hiddens)


def scores_of(query, keys):
    return lax.dot_general(query, keys, (((1,), (1,)), ((), ())), preferred_element_type=jnp.float32)


def attend_own_kernel(q_ref, own_ref, top, acc):
    for tile in range(4):
        rows = pl.ds(tile * TILE, TILE)
        first = 0 if tile < 2 else tile * TILE
        count = (tile + 1) * TILE - first
        query_pos = tile * TILE - first + lax.broadcasted_iota(jnp.int32, (TILE, count), 0)
        key_pos = lax.broadcasted_iota(jnp.int32, (TILE, count), 1)
        allowed = key_pos <= query_pos
        if tile >= 2:
            allowed &= (key_pos >> 2) == (query_pos >> 2)
        scores = scores_of(q_ref[rows, :], own_ref[pl.ds(first, count), :HD])
        scores = jnp.where(allowed, scores, NEG)
        best = jnp.max(scores, axis=1, keepdims=True)
        weights = jnp.exp2((scores - best) * SCALE).astype(jnp.bfloat16)
        own_vals = jnp.concatenate(
            [own_ref[pl.ds(first, count), HD:], jnp.ones((count, HD), jnp.bfloat16)], axis=1
        )
        acc[rows, :] = jnp.dot(weights, own_vals, preferred_element_type=jnp.float32)
        top[rows, :] = jnp.broadcast_to(best, (TILE, HD))


STATE = (
    jax.ShapeDtypeStruct((ROWS, HD), jnp.float32),
    jax.ShapeDtypeStruct((ROWS, 2 * HD), jnp.float32),
)


def attend_own(query, own):
    return pl.pallas_call(
        attend_own_kernel,
        out_shape=STATE,
        in_specs=[VMEM] * 2,
        out_specs=(VMEM, VMEM),
        compiler_params=pltpu.CompilerParams(vmem_limit_bytes=8 * MIB),
        cost_estimate=pl.CostEstimate(
            flops=4 * ROWS * 512 * 256, bytes_accessed=2 * MIB, transcendentals=ROWS * 384
        ),
        name="attend_own",
    )(query, own)


def attend_block_kernel(last, q_ref, bias_ref, pos_ref, len_ref, kv_ref, top_in, acc_in, *rest):
    if last:
        out_ref, keys, vals = rest
    else:
        top_out, acc_out, keys, vals = rest
    block = kv_ref.shape[0]
    row_page = lax.broadcasted_iota(jnp.int32, (block, HD), 0) >> 4
    column = lax.broadcasted_iota(jnp.int32, (block, HD), 1)
    keys[:, :HD] = kv_ref[:, :HD]
    keys[:, HD:] = jnp.where(row_page == column, 1.0, 0.0).astype(jnp.bfloat16)
    vals[:, :HD] = kv_ref[:, HD:]
    vals[:, HD:] = jnp.ones((block, HD), jnp.bfloat16)

    for tile in range(4):
        rows = pl.ds(tile * TILE, TILE)
        query = jnp.concatenate([q_ref[rows, :], bias_ref[rows, :]], axis=1)
        scores = scores_of(query, keys[...])
        if tile >= 2:
            length = len_ref[pl.ds((tile - 2) * TILE, TILE), :]
            scores = jnp.where(pos_ref[...] < length, scores, NEG)
        before = top_in[rows, :1]
        best = jnp.maximum(before, jnp.max(scores, axis=1, keepdims=True))
        weights = jnp.exp2((scores - best) * SCALE).astype(jnp.bfloat16)
        summed = jnp.dot(weights, vals[...], preferred_element_type=jnp.float32)
        state = acc_in[rows, :] * jnp.exp2((before - best) * SCALE) + summed
        if last:
            out_ref[rows, :] = (state[:, :HD] / state[:, HD:]).astype(jnp.bfloat16)
        else:
            acc_out[rows, :] = state
            top_out[rows, :] = jnp.broadcast_to(best, (TILE, HD))


def attend_block(state, query, bias, pos, lengths, block, last=False):
    count = block.shape[0]
    return pl.pallas_call(
        functools.partial(attend_block_kernel, last),
        out_shape=jax.ShapeDtypeStruct((ROWS, HD), jnp.bfloat16) if last else STATE,
        in_specs=[VMEM] * 7,
        out_specs=VMEM if last else (VMEM, VMEM),
        scratch_shapes=[pltpu.VMEM((count, 2 * HD), jnp.bfloat16)] * 2,
        compiler_params=pltpu.CompilerParams(vmem_limit_bytes=20 * MIB),
        cost_estimate=pl.CostEstimate(
            flops=4 * ROWS * count * 256, bytes_accessed=4 * MIB, transcendentals=ROWS * count
        ),
        name="attend_last" if last else "attend_block",
    )(query, bias, pos, lengths, block, *state)


def on_device(hidden, w_query, w_key, w_value, prompt_len, page_table):
    g, z, y, c, x = (lax.axis_index(name) for name in ("g", "z", "y", "c", "x"))
    local = hidden[0]

    with jax.named_scope("weights"):
        def head_of(head):
            pieces = [lax.dynamic_slice_in_dim(w, head * HD, HD, 1) for w in (w_key, w_value, w_query)]
            return jnp.concatenate(pieces, axis=1)

        mine = head_of(2 * g + c)
        other = shift(head_of(2 * g + 1 - c), "c", 1)
        both = jnp.where(c == 0, jnp.concatenate([mine, other]), jnp.concatenate([other, mine]))
        quarter = shift(lax.dynamic_slice_in_dim(local, x * 64, 64, 0), "g", 1)
        quarter, both = after(quarter, both)
        column, row = after(ring(both, "z"), ring(both, "y"))
        weights = row + ring_halves(jnp.concatenate(column[1:], axis=0), "y")

    with jax.named_scope("hidden"):
        remote = lax.all_gather(quarter, ("c", "x"), axis=0, tiled=True)
        hiddens = (local, shift(local, "c", 1), remote)

    with jax.named_scope("tables"):
        def chips_of(dz, dy):
            return ((z + jnp.array(dz)) % 4) * 4 + (y + jnp.array(dy)) % 4

        own_y = chips_of([0, 0, 0, 0], [0, 1, 2, 3])
        rest = [chips_of([1, 2, 3], [k, k, k]) for k in range(4)]
        halves = (jnp.concatenate([own_y] + rest)[:, None] * 2 + jnp.arange(2)).reshape(-1)
        places = jnp.stack([2 * g + c, 2 * g + 1 - c, 2 * (1 - g)])
        table = jnp.concatenate([halves, places]).astype(jnp.int32)
        per_chunk = CHUNK // PAGE
        order = [own_y] + [jnp.concatenate([rest[k], jnp.full((1,), -1, jnp.int32)]) for k in range(4)]
        order = jnp.concatenate(order).astype(jnp.int32)
        pages = (order[:, None] * per_chunk + jnp.arange(per_chunk)[None, :]).reshape(-1)
        pos = (pages[:, None] * PAGE + jnp.arange(PAGE)[None, :]).reshape(5, 1, HD * PAGE).astype(jnp.int32)
        chip = z * 4 + y
        row_count = CHUNK // STEPS
        own_table = lax.dynamic_slice_in_dim(page_table, chip * row_count, row_count, 0)
        own_len = lax.dynamic_slice_in_dim(prompt_len, chip * row_count, row_count, 0)
        listed = jnp.any(own_table[:, :, None] == pages[None, None, :], axis=1)
        listed &= pages[None, :] * PAGE < own_len[:, None]
        listed = jnp.repeat(listed, STEPS, axis=0)
        lengths = jnp.repeat(own_len, STEPS)[:, None]
        earlier = jnp.broadcast_to((pages // per_chunk < chip)[None, :], listed.shape)
        bias = jnp.where(jnp.concatenate([earlier, listed]), 0.0, NEG).astype(jnp.bfloat16)

    own, query = project(table, hiddens, weights)
    with jax.named_scope("cache"):
        prompt = own[:CHUNK]
        column, row = after(ring(prompt, "z"), ring(prompt, "y"))
        near = jnp.concatenate(row, axis=0)
        far = ring_halves(jnp.concatenate(column[1:], axis=0), "y")
        far = [far[0], far[1], jnp.concatenate(far[2:4], axis=0), far[4]]
    state = attend_own(query, own)
    for k, block in ((0, near), (1, far[0]), (2, far[1]), (4, far[3]), (3, far[2])):
        state = attend_block(
            state, query, bias[:, k * HD:(k + 1) * HD], pos[k, :, :block.shape[0]], lengths, block, k == 3
        )
    out = state

    with jax.named_scope("output"):
        tiles = out.reshape(2, 2, TILE, HD)
        kept = lax.dynamic_index_in_dim(tiles, c, 1, False)
        swapped = shift(lax.dynamic_index_in_dim(tiles, 1 - c, 1, False), "c", 1)
        pair = jnp.where(c == 0, jnp.concatenate([kept, swapped], 2), jnp.concatenate([swapped, kept], 2))
        stay = lax.dynamic_index_in_dim(pair, g, 0, False)
        come = shift(lax.dynamic_index_in_dim(pair, 1 - g, 0, False), "g", 1)
        result = jnp.where(g == 0, jnp.concatenate([stay, come], 1), jnp.concatenate([come, stay], 1))
    return result[None]


def solution(mesh):
    names = ("g", "z", "y", "c", "x")
    split = Mesh(mesh.devices.reshape([SIZES[name] for name in names]), names)
    weight = P(("z", "y", "c"), "x")
    return jax.shard_map(
        on_device,
        mesh=split,
        in_specs=(P("g", ("z", "y", "c"), None), weight, weight, weight, P(), P()),
        out_specs=P("g", ("z", "y", "c"), "x"),
        check_vma=False,
    )
```

```python
import functools

import jax
import jax.numpy as jnp
from jax import lax
from jax.experimental import pallas as pl
from jax.experimental.pallas import tpu as pltpu
from jax.sharding import Mesh, PartitionSpec as P

HD = 128
PAGE = 16
STEPS = 4
NEG = -1e30
SCALE = HD ** -0.5 * 1.4426950408889634
SIZES = {"g": 2, "z": 4, "y": 4, "c": 2, "x": 4}
CHUNK = 512
TILE = 256
ROWS = 2 * CHUNK
MIB = 1024 * 1024
VMEM = pl.BlockSpec(memory_space=pltpu.VMEM)


def shift(value, axis, by):
    count = SIZES[axis]
    return lax.ppermute(value, axis, [((k + by) % count, k) for k in range(count)])


def together(*values):
    return lax.optimization_barrier(values)


def near_blocks(value):
    return [shift(value, "z", k) for k in (1, 2, 3)] + [shift(value, "y", k) for k in (1, 3)]


def far_blocks(blocks, *beside):
    rows = blocks[0].shape[0]
    column = jnp.concatenate(blocks[:3], axis=0)
    near, back, *beside = together(shift(column, "y", 1), shift(column, "y", 3), *beside)
    half_a = shift(jnp.concatenate([blocks[3], near[:rows]], axis=0), "y", 1)
    half_b = shift(back[rows:], "y", 3)
    return [near, back, half_a, half_b] + beside


def dot(left, right):
    return jnp.dot(left, right, preferred_element_type=jnp.float32).astype(jnp.bfloat16)


def project_prompt_kernel(table, *refs):
    pieces, hiddens = refs[:10], refs[10:14]
    kv_out, w_all = refs[14:]
    place = 0
    for piece in pieces:
        for start in range(0, piece.shape[0], 256):
            rows = pl.ds(pl.multiple_of(table[place] * 256, 256), 256)
            w_all[rows, :] = piece[pl.ds(start, 256), :]
            place += 1
    for group in range(2):
        @pl.when(table[16] == group)
        def own_group():
            for k in range(2):
                rows = pl.ds(pl.multiple_of(table[17 + k] * 256, 256), 256)
                kv_out[rows, :] = dot(hiddens[2 * group + k][...], w_all[:, :2 * HD])


def project_rest_kernel(table, w_all, *refs):
    hiddens = refs[:4]
    kv_out, q_out = refs[4:]
    for group in range(2):
        @pl.when(table[16] == group)
        def own_group():
            for k in range(2):
                start = pl.multiple_of(table[17 + k] * 256, 256)
                q_out[pl.ds(start, 256), :] = dot(hiddens[2 * group + k][...], w_all[:, 2 * HD:])
                result = dot(hiddens[2 - 2 * group + k][...], w_all[...])
                kv_out[pl.ds(start, 256), :] = result[:, :2 * HD]
                q_out[pl.ds(CHUNK + start, 256), :] = result[:, 2 * HD:]


def project_prompt(table, hiddens, pieces):
    return pl.pallas_call(
        project_prompt_kernel,
        out_shape=(
            jax.ShapeDtypeStruct((CHUNK, 2 * HD), jnp.bfloat16),
            jax.ShapeDtypeStruct((4096, 3 * HD), jnp.bfloat16),
        ),
        in_specs=[pl.BlockSpec(memory_space=pltpu.SMEM)] + [VMEM] * 14,
        out_specs=(VMEM, VMEM),
        compiler_params=pltpu.CompilerParams(vmem_limit_bytes=8 * MIB),
        cost_estimate=pl.CostEstimate(
            flops=4 * CHUNK * 4096 * 256, bytes_accessed=8 * MIB, transcendentals=0
        ),
        name="project_prompt",
    )(table, *pieces, *hiddens)


def project_rest(table, hiddens, weights):
    return pl.pallas_call(
        project_rest_kernel,
        out_shape=(
            jax.ShapeDtypeStruct((CHUNK, 2 * HD), jnp.bfloat16),
            jax.ShapeDtypeStruct((ROWS, HD), jnp.bfloat16),
        ),
        in_specs=[pl.BlockSpec(memory_space=pltpu.SMEM)] + [VMEM] * 5,
        out_specs=(VMEM, VMEM),
        compiler_params=pltpu.CompilerParams(vmem_limit_bytes=8 * MIB),
        cost_estimate=pl.CostEstimate(
            flops=4 * ROWS * 4096 * 256, bytes_accessed=8 * MIB, transcendentals=0
        ),
        name="project_rest",
    )(table, weights, *hiddens)


def scores_of(query, keys):
    return lax.dot_general(query, keys, (((1,), (1,)), ((), ())), preferred_element_type=jnp.float32)


def attend_own_kernel(q_ref, prompt_ref, fresh_ref, top, acc):
    for tile in range(4):
        rows = pl.ds(tile * TILE, TILE)
        own_ref = prompt_ref if tile < 2 else fresh_ref
        first = 0 if tile < 2 else (tile - 2) * TILE
        count = (tile % 2 + 1) * TILE - first
        query_pos = tile % 2 * TILE - first + lax.broadcasted_iota(jnp.int32, (TILE, count), 0)
        key_pos = lax.broadcasted_iota(jnp.int32, (TILE, count), 1)
        allowed = key_pos <= query_pos
        if tile >= 2:
            allowed &= (key_pos >> 2) == (query_pos >> 2)
        scores = scores_of(q_ref[rows, :], own_ref[pl.ds(first, count), :HD])
        scores = jnp.where(allowed, scores, NEG)
        best = jnp.max(scores, axis=1, keepdims=True)
        weights = jnp.exp2((scores - best) * SCALE).astype(jnp.bfloat16)
        own_vals = jnp.concatenate(
            [own_ref[pl.ds(first, count), HD:], jnp.ones((count, HD), jnp.bfloat16)], axis=1
        )
        acc[rows, :] = jnp.dot(weights, own_vals, preferred_element_type=jnp.float32)
        top[rows, :] = jnp.broadcast_to(best, (TILE, HD))


STATE = (
    jax.ShapeDtypeStruct((ROWS, HD), jnp.float32),
    jax.ShapeDtypeStruct((ROWS, 2 * HD), jnp.float32),
)


def attend_own(query, prompt, fresh):
    return pl.pallas_call(
        attend_own_kernel,
        out_shape=STATE,
        in_specs=[VMEM] * 3,
        out_specs=(VMEM, VMEM),
        compiler_params=pltpu.CompilerParams(vmem_limit_bytes=8 * MIB),
        cost_estimate=pl.CostEstimate(
            flops=4 * ROWS * 512 * 256, bytes_accessed=2 * MIB, transcendentals=ROWS * 384
        ),
        name="attend_own",
    )(query, prompt, fresh)


def attend_block_kernel(count, last, q_ref, bias_ref, pos_ref, len_ref, top_in, acc_in, *rest):
    pieces, rest = rest[:count], rest[count:]
    if last:
        out_ref, keys, vals = rest
    else:
        top_out, acc_out, keys, vals = rest
    block = keys.shape[0]
    row_page = lax.broadcasted_iota(jnp.int32, (block, HD), 0) >> 4
    column = lax.broadcasted_iota(jnp.int32, (block, HD), 1)
    start = 0
    for piece in pieces:
        part = pl.ds(start, piece.shape[0])
        keys[part, :HD] = piece[:, :HD]
        vals[part, :HD] = piece[:, HD:]
        start += piece.shape[0]
    keys[:, HD:] = jnp.where(row_page == column, 1.0, 0.0).astype(jnp.bfloat16)
    vals[:, HD:] = jnp.ones((block, HD), jnp.bfloat16)

    for tile in range(4):
        rows = pl.ds(tile * TILE, TILE)
        query = jnp.concatenate([q_ref[rows, :], bias_ref[rows, :]], axis=1)
        scores = scores_of(query, keys[...])
        if tile >= 2:
            length = len_ref[pl.ds((tile - 2) * TILE, TILE), :]
            scores = jnp.where(pos_ref[...] < length, scores, NEG)
        before = top_in[rows, :1]
        best = jnp.maximum(before, jnp.max(scores, axis=1, keepdims=True))
        weights = jnp.exp2((scores - best) * SCALE).astype(jnp.bfloat16)
        summed = jnp.dot(weights, vals[...], preferred_element_type=jnp.float32)
        state = acc_in[rows, :] * jnp.exp2((before - best) * SCALE) + summed
        if last:
            out_ref[rows, :] = (state[:, :HD] / state[:, HD:]).astype(jnp.bfloat16)
        else:
            acc_out[rows, :] = state
            top_out[rows, :] = jnp.broadcast_to(best, (TILE, HD))


def attend_block(state, query, bias, pos, lengths, pieces, last=False):
    count = sum(piece.shape[0] for piece in pieces)
    return pl.pallas_call(
        functools.partial(attend_block_kernel, len(pieces), last),
        out_shape=jax.ShapeDtypeStruct((ROWS, HD), jnp.bfloat16) if last else STATE,
        in_specs=[VMEM] * (6 + len(pieces)),
        out_specs=VMEM if last else (VMEM, VMEM),
        scratch_shapes=[pltpu.VMEM((count, 2 * HD), jnp.bfloat16)] * 2,
        compiler_params=pltpu.CompilerParams(vmem_limit_bytes=20 * MIB),
        cost_estimate=pl.CostEstimate(
            flops=4 * ROWS * count * 256, bytes_accessed=4 * MIB, transcendentals=ROWS * count
        ),
        name="attend_last" if last else "attend_block",
    )(query, bias, pos, lengths, *state, *pieces)


def on_device(hidden, w_query, w_key, w_value, prompt_len, page_table):
    g, z, y, c, x = (lax.axis_index(name) for name in ("g", "z", "y", "c", "x"))
    local = hidden[0]

    with jax.named_scope("weights"):
        def head_of(head):
            pieces = [lax.dynamic_slice_in_dim(w, head * HD, HD, 1) for w in (w_key, w_value, w_query)]
            return jnp.concatenate(pieces, axis=1)

        quarter = shift(lax.dynamic_slice_in_dim(local, x * 64, 64, 0), "g", 1)
        mine = head_of(2 * g + c)
        other = shift(head_of(2 * g + 1 - c), "c", 1)
        both = jnp.where(c == 0, jnp.concatenate([mine, other]), jnp.concatenate([other, mine]))
        quarter, both, local_other = together(quarter, both, shift(local, "c", 1))
        *blocks, quarter_1, quarter_3 = together(
            *near_blocks(both), shift(quarter, "x", 1), shift(quarter, "x", 3)
        )

    with jax.named_scope("hidden"):
        remote = jnp.zeros_like(local)
        for place, piece in (
            (x, quarter),
            ((x + 1) % 4, quarter_1),
            ((x + 3) % 4, quarter_3),
        ):
            remote = lax.dynamic_update_slice_in_dim(remote, piece, place * 64, 0)
        *far, low, high = far_blocks(blocks, shift(quarter_1[:32], "x", 1), shift(quarter_3[32:], "x", 3))
        pieces = [both] + blocks + far
        opposite = jnp.concatenate([low, high])
        remote = lax.dynamic_update_slice_in_dim(remote, opposite, (x + 2) % 4 * 64, 0)
        hiddens = (local, local_other, remote, shift(remote, "c", 1))

    with jax.named_scope("tables"):
        def chips_of(dz, dy):
            return ((z + jnp.array(dz)) % 4) * 4 + (y + jnp.array(dy)) % 4

        first = chips_of([0, 0, 0], [0, 1, 3])
        column, near, back = [chips_of([1, 2, 3], [k, k, k]) for k in (0, 1, 3)]
        opposite = chips_of([0, 1, 2, 3], [2, 2, 2, 2])
        places = jnp.stack([g, c, 1 - c])
        table = jnp.concatenate([first[:1], column, first[1:], near, back, opposite, places]).astype(jnp.int32)
        per_chunk = CHUNK // PAGE
        pad = jnp.full((1,), -1, jnp.int32)
        order = jnp.concatenate([first, pad, column, pad, near, pad, back, pad, opposite]).astype(jnp.int32)
        pages = (order[:, None] * per_chunk + jnp.arange(per_chunk)[None, :]).reshape(-1)
        pos = (pages[:, None] * PAGE + jnp.arange(PAGE)[None, :]).reshape(5, 1, HD * PAGE).astype(jnp.int32)
        chip = z * 4 + y
        row_count = CHUNK // STEPS
        own_table = lax.dynamic_slice_in_dim(page_table, chip * row_count, row_count, 0)
        own_len = lax.dynamic_slice_in_dim(prompt_len, chip * row_count, row_count, 0)
        listed = jnp.any(own_table[:, :, None] == pages[None, None, :], axis=1)
        listed &= pages[None, :] * PAGE < own_len[:, None]
        listed = jnp.repeat(listed, STEPS, axis=0)
        lengths = jnp.repeat(own_len, STEPS)[:, None]
        earlier = jnp.broadcast_to((pages // per_chunk < chip)[None, :], listed.shape)
        bias = jnp.where(jnp.concatenate([earlier, listed]), 0.0, NEG).astype(jnp.bfloat16)

    prompt, weights = project_prompt(table, hiddens, pieces)
    fresh, query = project_rest(table, hiddens, weights)

    def attend_parts(k, state, parts):
        keys = sum(part.shape[0] for part in parts)
        return attend_block(
            state, query, bias[:, k * HD:(k + 1) * HD], pos[k, :, :keys], lengths, parts, k == 4
        )

    with jax.named_scope("cache"):
        *blocks, fresh, query = together(*near_blocks(prompt), fresh, query)
        state = attend_own(query, prompt, fresh)
        state = attend_parts(0, state, [prompt, blocks[3], blocks[4]])
        state = attend_parts(1, state, blocks[:3])
        near, back, half_a, half_b, *state = far_blocks(blocks, *state)
        state = attend_parts(2, state, [near])
        state = attend_parts(3, state, [back])
        state = attend_parts(4, state, [half_a, half_b])
    out = state

    with jax.named_scope("output"):
        tiles = out.reshape(2, 2, TILE, HD)
        kept = lax.dynamic_index_in_dim(tiles, c, 1, False)
        swapped = shift(lax.dynamic_index_in_dim(tiles, 1 - c, 1, False), "c", 1)
        pair = jnp.where(c == 0, jnp.concatenate([kept, swapped], 2), jnp.concatenate([swapped, kept], 2))
        stay = lax.dynamic_index_in_dim(pair, g, 0, False)
        come = shift(lax.dynamic_index_in_dim(pair, 1 - g, 0, False), "g", 1)
        result = jnp.where(g == 0, jnp.concatenate([stay, come], 1), jnp.concatenate([come, stay], 1))
    return result[None]


def solution(mesh):
    names = ("g", "z", "y", "c", "x")
    split = Mesh(mesh.devices.reshape([SIZES[name] for name in names]), names)
    weight = P(("z", "y", "c"), "x")
    return jax.shard_map(
        on_device,
        mesh=split,
        in_specs=(P("g", ("z", "y", "c"), None), weight, weight, weight, P(), P()),
        out_specs=P("g", ("z", "y", "c"), "x"),
        check_vma=False,
    )
```

```python
import functools

import jax
import jax.numpy as jnp
from jax import lax
from jax.experimental import pallas as pl
from jax.experimental.pallas import tpu as pltpu
from jax.sharding import Mesh, PartitionSpec as P

HD = 128
PAGE = 16
STEPS = 4
NEG = -1e30
SCALE = HD ** -0.5 * 1.4426950408889634
SIZES = {"g": 2, "z": 4, "y": 4, "c": 2, "x": 4}
CHUNK = 512
TILE = 256
ROWS = 2 * CHUNK
MIB = 1024 * 1024
VMEM = pl.BlockSpec(memory_space=pltpu.VMEM)


def shift(value, axis, by):
    count = SIZES[axis]
    return lax.ppermute(value, axis, [((k + by) % count, k) for k in range(count)])


def together(*values):
    return lax.optimization_barrier(values)


def near_blocks(value):
    return [shift(value, "z", k) for k in (1, 2, 3)] + [shift(value, "y", k) for k in (1, 3)]


def side_columns(blocks, *beside):
    column = jnp.concatenate(blocks[:3], axis=0)
    near, back, *beside = together(shift(column, "y", 1), shift(column, "y", 3), *beside)
    return [near, back], beside


def opposite_halves(blocks, sides):
    rows = blocks[0].shape[0]
    half_a = shift(jnp.concatenate([blocks[3], sides[0][:rows]], axis=0), "y", 1)
    return [half_a, shift(sides[1][rows:], "y", 3)]


def dot(left, right):
    return jnp.dot(left, right, preferred_element_type=jnp.float32).astype(jnp.bfloat16)


def project_prompt_kernel(table, *refs):
    pieces, hiddens = refs[:10], refs[10:14]
    kv_out, w_all = refs[14:]
    place = 0
    for piece in pieces:
        for start in range(0, piece.shape[0], 256):
            rows = pl.ds(pl.multiple_of(table[place] * 256, 256), 256)
            w_all[rows, :] = piece[pl.ds(start, 256), :]
            place += 1
    for group in range(2):
        @pl.when(table[16] == group)
        def own_group():
            for k in range(2):
                rows = pl.ds(pl.multiple_of(table[17 + k] * 256, 256), 256)
                kv_out[rows, :] = dot(hiddens[2 * group + k][...], w_all[:, :2 * HD])


def project_rest_kernel(table, w_all, *refs):
    hiddens = refs[:4]
    kv_out, q_out = refs[4:]
    for group in range(2):
        @pl.when(table[16] == group)
        def own_group():
            for k in range(2):
                start = pl.multiple_of(table[17 + k] * 256, 256)
                q_out[pl.ds(start, 256), :] = dot(hiddens[2 * group + k][...], w_all[:, 2 * HD:])
                result = dot(hiddens[2 - 2 * group + k][...], w_all[...])
                kv_out[pl.ds(start, 256), :] = result[:, :2 * HD]
                q_out[pl.ds(CHUNK + start, 256), :] = result[:, 2 * HD:]


def project_prompt(table, hiddens, pieces):
    return pl.pallas_call(
        project_prompt_kernel,
        out_shape=(
            jax.ShapeDtypeStruct((CHUNK, 2 * HD), jnp.bfloat16),
            jax.ShapeDtypeStruct((4096, 3 * HD), jnp.bfloat16),
        ),
        in_specs=[pl.BlockSpec(memory_space=pltpu.SMEM)] + [VMEM] * 14,
        out_specs=(VMEM, VMEM),
        compiler_params=pltpu.CompilerParams(vmem_limit_bytes=8 * MIB),
        cost_estimate=pl.CostEstimate(
            flops=4 * CHUNK * 4096 * 256, bytes_accessed=8 * MIB, transcendentals=0
        ),
        name="project_prompt",
    )(table, *pieces, *hiddens)


def project_rest(table, hiddens, weights):
    return pl.pallas_call(
        project_rest_kernel,
        out_shape=(
            jax.ShapeDtypeStruct((CHUNK, 2 * HD), jnp.bfloat16),
            jax.ShapeDtypeStruct((ROWS, HD), jnp.bfloat16),
        ),
        in_specs=[pl.BlockSpec(memory_space=pltpu.SMEM)] + [VMEM] * 5,
        out_specs=(VMEM, VMEM),
        compiler_params=pltpu.CompilerParams(vmem_limit_bytes=8 * MIB),
        cost_estimate=pl.CostEstimate(
            flops=4 * ROWS * 4096 * 256, bytes_accessed=8 * MIB, transcendentals=0
        ),
        name="project_rest",
    )(table, weights, *hiddens)


def scores_of(query, keys):
    return lax.dot_general(query, keys, (((1,), (1,)), ((), ())), preferred_element_type=jnp.float32)


def attend_own_kernel(q_ref, prompt_ref, fresh_ref, top, acc):
    for tile in range(4):
        rows = pl.ds(tile * TILE, TILE)
        own_ref = prompt_ref if tile < 2 else fresh_ref
        first = 0 if tile < 2 else (tile - 2) * TILE
        count = (tile % 2 + 1) * TILE - first
        query_pos = tile % 2 * TILE - first + lax.broadcasted_iota(jnp.int32, (TILE, count), 0)
        key_pos = lax.broadcasted_iota(jnp.int32, (TILE, count), 1)
        allowed = key_pos <= query_pos
        if tile >= 2:
            allowed &= (key_pos >> 2) == (query_pos >> 2)
        scores = scores_of(q_ref[rows, :], own_ref[pl.ds(first, count), :HD])
        scores = jnp.where(allowed, scores, NEG)
        best = jnp.max(scores, axis=1, keepdims=True)
        weights = jnp.exp2((scores - best) * SCALE).astype(jnp.bfloat16)
        own_vals = jnp.concatenate(
            [own_ref[pl.ds(first, count), HD:], jnp.ones((count, HD), jnp.bfloat16)], axis=1
        )
        acc[rows, :] = jnp.dot(weights, own_vals, preferred_element_type=jnp.float32)
        top[rows, :] = jnp.broadcast_to(best, (TILE, HD))


STATE = (
    jax.ShapeDtypeStruct((ROWS, HD), jnp.float32),
    jax.ShapeDtypeStruct((ROWS, 2 * HD), jnp.float32),
)


def attend_own(query, prompt, fresh):
    return pl.pallas_call(
        attend_own_kernel,
        out_shape=STATE,
        in_specs=[VMEM] * 3,
        out_specs=(VMEM, VMEM),
        compiler_params=pltpu.CompilerParams(vmem_limit_bytes=8 * MIB),
        cost_estimate=pl.CostEstimate(
            flops=4 * ROWS * 512 * 256, bytes_accessed=2 * MIB, transcendentals=ROWS * 384
        ),
        name="attend_own",
    )(query, prompt, fresh)


def attend_block_kernel(count, last, q_ref, bias_ref, pos_ref, len_ref, top_in, acc_in, *rest):
    pieces, rest = rest[:count], rest[count:]
    if last:
        out_ref, keys, vals = rest
    else:
        top_out, acc_out, keys, vals = rest
    block = keys.shape[0]
    row_page = lax.broadcasted_iota(jnp.int32, (block, HD), 0) >> 4
    column = lax.broadcasted_iota(jnp.int32, (block, HD), 1)
    start = 0
    for piece in pieces:
        part = pl.ds(start, piece.shape[0])
        keys[part, :HD] = piece[:, :HD]
        vals[part, :HD] = piece[:, HD:]
        start += piece.shape[0]
    keys[:, HD:] = jnp.where(row_page == column, 1.0, 0.0).astype(jnp.bfloat16)
    vals[:, HD:] = jnp.ones((block, HD), jnp.bfloat16)

    for tile in range(4):
        rows = pl.ds(tile * TILE, TILE)
        query = jnp.concatenate([q_ref[rows, :], bias_ref[rows, :]], axis=1)
        scores = scores_of(query, keys[...])
        if tile >= 2:
            length = len_ref[pl.ds((tile - 2) * TILE, TILE), :]
            scores = jnp.where(pos_ref[...] < length, scores, NEG)
        before = top_in[rows, :1]
        best = jnp.maximum(before, jnp.max(scores, axis=1, keepdims=True))
        weights = jnp.exp2((scores - best) * SCALE).astype(jnp.bfloat16)
        summed = jnp.dot(weights, vals[...], preferred_element_type=jnp.float32)
        state = acc_in[rows, :] * jnp.exp2((before - best) * SCALE) + summed
        if last:
            out_ref[rows, :] = (state[:, :HD] / state[:, HD:]).astype(jnp.bfloat16)
        else:
            acc_out[rows, :] = state
            top_out[rows, :] = jnp.broadcast_to(best, (TILE, HD))


def attend_block(state, query, bias, pos, lengths, pieces, last=False):
    count = sum(piece.shape[0] for piece in pieces)
    return pl.pallas_call(
        functools.partial(attend_block_kernel, len(pieces), last),
        out_shape=jax.ShapeDtypeStruct((ROWS, HD), jnp.bfloat16) if last else STATE,
        in_specs=[VMEM] * (6 + len(pieces)),
        out_specs=VMEM if last else (VMEM, VMEM),
        scratch_shapes=[pltpu.VMEM((count, 2 * HD), jnp.bfloat16)] * 2,
        compiler_params=pltpu.CompilerParams(vmem_limit_bytes=20 * MIB),
        cost_estimate=pl.CostEstimate(
            flops=4 * ROWS * count * 256, bytes_accessed=4 * MIB, transcendentals=ROWS * count
        ),
        name="attend_last" if last else "attend_block",
    )(query, bias, pos, lengths, *state, *pieces)


def on_device(hidden, w_query, w_key, w_value, prompt_len, page_table):
    g, z, y, c, x = (lax.axis_index(name) for name in ("g", "z", "y", "c", "x"))
    local = hidden[0]

    with jax.named_scope("weights"):
        def head_of(head):
            pieces = [lax.dynamic_slice_in_dim(w, head * HD, HD, 1) for w in (w_key, w_value, w_query)]
            return jnp.concatenate(pieces, axis=1)

        quarter = shift(lax.dynamic_slice_in_dim(local, x * 64, 64, 0), "g", 1)
        mine = head_of(2 * g + c)
        other, page_table, prompt_len = together(shift(head_of(2 * g + 1 - c), "c", 1), page_table, prompt_len)
        both = jnp.where(c == 0, jnp.concatenate([mine, other]), jnp.concatenate([other, mine]))

    with jax.named_scope("tables"):
        def chips_of(dz, dy):
            return ((z + jnp.array(dz)) % 4) * 4 + (y + jnp.array(dy)) % 4

        first = chips_of([0, 0, 0], [0, 1, 3])
        column, near, back = [chips_of([1, 2, 3], [k, k, k]) for k in (0, 1, 3)]
        opposite = chips_of([0, 1, 2, 3], [2, 2, 2, 2])
        places = jnp.stack([g, c, 1 - c])
        table = jnp.concatenate([first[:1], column, first[1:], near, back, opposite, places]).astype(jnp.int32)
        per_chunk = CHUNK // PAGE
        pad = jnp.full((1,), -1, jnp.int32)
        order = jnp.concatenate([first, pad, column, pad, near, pad, back, pad, opposite]).astype(jnp.int32)
        pages = (order[:, None] * per_chunk + jnp.arange(per_chunk)[None, :]).reshape(-1)
        pos = (pages[:, None] * PAGE + jnp.arange(PAGE)[None, :]).reshape(5, 1, HD * PAGE).astype(jnp.int32)
        chip = z * 4 + y
        row_count = CHUNK // STEPS
        own_table = lax.dynamic_slice_in_dim(page_table, chip * row_count, row_count, 0)
        own_len = lax.dynamic_slice_in_dim(prompt_len, chip * row_count, row_count, 0)
        listed = jnp.any(own_table[:, :, None] == pages[None, None, :], axis=1)
        listed &= pages[None, :] * PAGE < own_len[:, None]
        listed = jnp.repeat(listed, STEPS, axis=0)
        lengths = jnp.repeat(own_len, STEPS)[:, None]
        earlier = jnp.broadcast_to((pages // per_chunk < chip)[None, :], listed.shape)
        bias = jnp.where(jnp.concatenate([earlier, listed]), 0.0, NEG).astype(jnp.bfloat16)

    with jax.named_scope("near_weights"):
        next_1, next_3, quarter, both, local_other, table, bias, pos, lengths = together(
            shift(both, "y", 1), shift(both, "y", 3), quarter, both, shift(local, "c", 1), table, bias, pos, lengths
        )
        *blocks, quarter_1, quarter_3 = together(
            *[shift(both, "z", k) for k in (1, 2, 3)], shift(quarter, "x", 1), shift(quarter, "x", 3)
        )
        blocks += [next_1, next_3]

    with jax.named_scope("hidden"):
        sides, (low, high) = side_columns(
            blocks, shift(quarter_1[:32], "x", 1), shift(quarter_3[32:], "x", 3)
        )
        pieces = [both] + blocks + sides + opposite_halves(blocks, sides)
        remote = jnp.zeros_like(local)
        for place, piece in (
            (x, quarter),
            ((x + 1) % 4, quarter_1),
            ((x + 3) % 4, quarter_3),
            ((x + 2) % 4, jnp.concatenate([low, high])),
        ):
            remote = lax.dynamic_update_slice_in_dim(remote, piece, place * 64, 0)
        hiddens = (local, local_other, remote, shift(remote, "c", 1))

    prompt, weights = project_prompt(table, hiddens, pieces)
    fresh, query = project_rest(table, hiddens, weights)

    def attend_parts(k, state, parts):
        keys = sum(part.shape[0] for part in parts)
        return attend_block(
            state, query, bias[:, k * HD:(k + 1) * HD], pos[k, :, :keys], lengths, parts, k == 4
        )

    with jax.named_scope("cache"):
        *blocks, fresh, query = together(*near_blocks(prompt), fresh, query)
        state = attend_own(query, prompt, fresh)
        state = attend_parts(0, state, [prompt, blocks[3], blocks[4]])
        state = attend_parts(1, state, blocks[:3])
        sides, state = side_columns(blocks, *state)
        halves = opposite_halves(blocks, sides)
        state = attend_parts(2, state, sides[:1])
        state = attend_parts(3, state, sides[1:])
        state = attend_parts(4, state, halves)
    out = state

    with jax.named_scope("output"):
        tiles = out.reshape(2, 2, TILE, HD)
        kept = lax.dynamic_index_in_dim(tiles, c, 1, False)
        swapped = shift(lax.dynamic_index_in_dim(tiles, 1 - c, 1, False), "c", 1)
        pair = jnp.where(c == 0, jnp.concatenate([kept, swapped], 2), jnp.concatenate([swapped, kept], 2))
        stay = lax.dynamic_index_in_dim(pair, g, 0, False)
        come = shift(lax.dynamic_index_in_dim(pair, 1 - g, 0, False), "g", 1)
        result = jnp.where(g == 0, jnp.concatenate([stay, come], 1), jnp.concatenate([come, stay], 1))
    return result[None]


def solution(mesh):
    names = ("g", "z", "y", "c", "x")
    split = Mesh(mesh.devices.reshape([SIZES[name] for name in names]), names)
    weight = P(("z", "y", "c"), "x")
    return jax.shard_map(
        on_device,
        mesh=split,
        in_specs=(P("g", ("z", "y", "c"), None), weight, weight, weight, P(), P()),
        out_specs=P("g", ("z", "y", "c"), "x"),
        check_vma=False,
    )
```

```python
import functools

import jax
import jax.numpy as jnp
from jax import lax
from jax.experimental import pallas as pl
from jax.experimental.pallas import tpu as pltpu
from jax.sharding import Mesh, PartitionSpec as P

HD = 128
PAGE = 16
STEPS = 4
NEG = -1e30
SCALE = HD ** -0.5 * 1.4426950408889634
SIZES = {"g": 2, "z": 4, "y": 4, "c": 2, "x": 4}
CHUNK = 512
TILE = 256
ROWS = 2 * CHUNK
MIB = 1024 * 1024
VMEM = pl.BlockSpec(memory_space=pltpu.VMEM)


def shift(value, axis, by):
    count = SIZES[axis]
    return lax.ppermute(value, axis, [((k + by) % count, k) for k in range(count)])


def together(*values):
    return lax.optimization_barrier(values)


def near_blocks(value):
    return [shift(value, "z", k) for k in (1, 2, 3)] + [shift(value, "y", k) for k in (1, 3)]


def side_columns(blocks, *beside):
    column = jnp.concatenate(blocks[:3], axis=0)
    near, back, *beside = together(shift(column, "y", 1), shift(column, "y", 3), *beside)
    return [near, back], beside


def opposite_halves(blocks, sides):
    rows = blocks[0].shape[0]
    half_a = shift(jnp.concatenate([blocks[3], sides[0][:rows]], axis=0), "y", 1)
    return [half_a, shift(sides[1][rows:], "y", 3)]


def dot(left, right):
    return jnp.dot(left, right, preferred_element_type=jnp.float32).astype(jnp.bfloat16)


HBM = pl.BlockSpec(memory_space=pltpu.HBM)
SMEM = pl.BlockSpec(memory_space=pltpu.SMEM)


def fetch(hiddens, buffer, sems):
    copies = [pltpu.make_async_copy(h, buffer.at[k], sems.at[k]) for k, h in enumerate(hiddens)]
    for item in copies:
        item.start()
    return copies


def project_prompt_kernel(table, *refs):
    pieces, hiddens = refs[:10], refs[10:14]
    kv_out, w_all, buffer, sems = refs[14:]
    for group in range(2):
        @pl.when(table[16] == group)
        def own_group():
            copies = fetch(hiddens[2 * group:2 * group + 2], buffer, sems)
            place = 0
            for piece in pieces:
                for start in range(0, piece.shape[0], 256):
                    rows = pl.ds(pl.multiple_of(table[place] * 256, 256), 256)
                    w_all[rows, :] = piece[pl.ds(start, 256), :]
                    place += 1
            for k in range(2):
                copies[k].wait()
                rows = pl.ds(pl.multiple_of(table[17 + k] * 256, 256), 256)
                kv_out[rows, :] = dot(buffer[k], w_all[:, :2 * HD])


def project_rest_kernel(table, w_all, *refs):
    hiddens = refs[:4]
    kv_out, q_out, buffer, sems = refs[4:]
    copies = fetch(hiddens, buffer, sems)
    for item in copies:
        item.wait()
    for group in range(2):
        @pl.when(table[16] == group)
        def own_group():
            for k in range(2):
                start = pl.multiple_of(table[17 + k] * 256, 256)
                q_out[pl.ds(start, 256), :] = dot(buffer[2 * group + k], w_all[:, 2 * HD:])
                result = dot(buffer[2 - 2 * group + k], w_all[...])
                kv_out[pl.ds(start, 256), :] = result[:, :2 * HD]
                q_out[pl.ds(CHUNK + start, 256), :] = result[:, 2 * HD:]


def project_prompt(table, hiddens, pieces):
    return pl.pallas_call(
        project_prompt_kernel,
        out_shape=(
            jax.ShapeDtypeStruct((CHUNK, 2 * HD), jnp.bfloat16),
            jax.ShapeDtypeStruct((4096, 3 * HD), jnp.bfloat16),
        ),
        in_specs=[SMEM] + [VMEM] * 10 + [HBM] * 4,
        out_specs=(VMEM, VMEM),
        scratch_shapes=[pltpu.VMEM((2, TILE, 4096), jnp.bfloat16), pltpu.SemaphoreType.DMA((2,))],
        compiler_params=pltpu.CompilerParams(vmem_limit_bytes=8 * MIB),
        cost_estimate=pl.CostEstimate(
            flops=4 * CHUNK * 4096 * 256, bytes_accessed=8 * MIB, transcendentals=0
        ),
        name="project_prompt",
    )(table, *pieces, *hiddens)


def project_rest(table, hiddens, weights):
    return pl.pallas_call(
        project_rest_kernel,
        out_shape=(
            jax.ShapeDtypeStruct((CHUNK, 2 * HD), jnp.bfloat16),
            jax.ShapeDtypeStruct((ROWS, HD), jnp.bfloat16),
        ),
        in_specs=[SMEM, VMEM] + [HBM] * 4,
        out_specs=(VMEM, VMEM),
        scratch_shapes=[pltpu.VMEM((4, TILE, 4096), jnp.bfloat16), pltpu.SemaphoreType.DMA((4,))],
        compiler_params=pltpu.CompilerParams(vmem_limit_bytes=12 * MIB),
        cost_estimate=pl.CostEstimate(
            flops=4 * ROWS * 4096 * 256, bytes_accessed=8 * MIB, transcendentals=0
        ),
        name="project_rest",
    )(table, weights, *hiddens)


def scores_of(query, keys):
    return lax.dot_general(query, keys, (((1,), (1,)), ((), ())), preferred_element_type=jnp.float32)


def attend_own_kernel(q_ref, prompt_ref, fresh_ref, top, acc):
    for tile in range(4):
        rows = pl.ds(tile * TILE, TILE)
        own_ref = prompt_ref if tile < 2 else fresh_ref
        first = 0 if tile < 2 else (tile - 2) * TILE
        count = (tile % 2 + 1) * TILE - first
        query_pos = tile % 2 * TILE - first + lax.broadcasted_iota(jnp.int32, (TILE, count), 0)
        key_pos = lax.broadcasted_iota(jnp.int32, (TILE, count), 1)
        allowed = key_pos <= query_pos
        if tile >= 2:
            allowed &= (key_pos >> 2) == (query_pos >> 2)
        scores = scores_of(q_ref[rows, :], own_ref[pl.ds(first, count), :HD])
        scores = jnp.where(allowed, scores, NEG)
        best = jnp.max(scores, axis=1, keepdims=True)
        weights = jnp.exp2((scores - best) * SCALE).astype(jnp.bfloat16)
        own_vals = jnp.concatenate(
            [own_ref[pl.ds(first, count), HD:], jnp.ones((count, HD), jnp.bfloat16)], axis=1
        )
        acc[rows, :] = jnp.dot(weights, own_vals, preferred_element_type=jnp.float32)
        top[rows, :] = jnp.broadcast_to(best, (TILE, HD))


STATE = (
    jax.ShapeDtypeStruct((ROWS, HD), jnp.float32),
    jax.ShapeDtypeStruct((ROWS, 2 * HD), jnp.float32),
)


def attend_own(query, prompt, fresh):
    return pl.pallas_call(
        attend_own_kernel,
        out_shape=STATE,
        in_specs=[VMEM] * 3,
        out_specs=(VMEM, VMEM),
        compiler_params=pltpu.CompilerParams(vmem_limit_bytes=8 * MIB),
        cost_estimate=pl.CostEstimate(
            flops=4 * ROWS * 512 * 256, bytes_accessed=2 * MIB, transcendentals=ROWS * 384
        ),
        name="attend_own",
    )(query, prompt, fresh)


def attend_block_kernel(count, last, q_ref, bias_ref, pos_ref, len_ref, top_in, acc_in, *rest):
    pieces, rest = rest[:count], rest[count:]
    if last:
        out_ref, keys, vals = rest
    else:
        top_out, acc_out, keys, vals = rest
    block = keys.shape[0]
    row_page = lax.broadcasted_iota(jnp.int32, (block, HD), 0) >> 4
    column = lax.broadcasted_iota(jnp.int32, (block, HD), 1)
    start = 0
    for piece in pieces:
        part = pl.ds(start, piece.shape[0])
        keys[part, :HD] = piece[:, :HD]
        vals[part, :HD] = piece[:, HD:]
        start += piece.shape[0]
    keys[:, HD:] = jnp.where(row_page == column, 1.0, 0.0).astype(jnp.bfloat16)
    vals[:, HD:] = jnp.ones((block, HD), jnp.bfloat16)

    for tile in range(4):
        rows = pl.ds(tile * TILE, TILE)
        query = jnp.concatenate([q_ref[rows, :], bias_ref[rows, :]], axis=1)
        scores = scores_of(query, keys[...])
        if tile >= 2:
            length = len_ref[pl.ds((tile - 2) * TILE, TILE), :]
            scores = jnp.where(pos_ref[...] < length, scores, NEG)
        before = top_in[rows, :1]
        best = jnp.maximum(before, jnp.max(scores, axis=1, keepdims=True))
        weights = jnp.exp2((scores - best) * SCALE).astype(jnp.bfloat16)
        summed = jnp.dot(weights, vals[...], preferred_element_type=jnp.float32)
        state = acc_in[rows, :] * jnp.exp2((before - best) * SCALE) + summed
        if last:
            out_ref[rows, :] = (state[:, :HD] / state[:, HD:]).astype(jnp.bfloat16)
        else:
            acc_out[rows, :] = state
            top_out[rows, :] = jnp.broadcast_to(best, (TILE, HD))


def attend_block(state, query, bias, pos, lengths, pieces, last=False):
    count = sum(piece.shape[0] for piece in pieces)
    return pl.pallas_call(
        functools.partial(attend_block_kernel, len(pieces), last),
        out_shape=jax.ShapeDtypeStruct((ROWS, HD), jnp.bfloat16) if last else STATE,
        in_specs=[VMEM] * (6 + len(pieces)),
        out_specs=VMEM if last else (VMEM, VMEM),
        scratch_shapes=[pltpu.VMEM((count, 2 * HD), jnp.bfloat16)] * 2,
        compiler_params=pltpu.CompilerParams(vmem_limit_bytes=20 * MIB),
        cost_estimate=pl.CostEstimate(
            flops=4 * ROWS * count * 256, bytes_accessed=4 * MIB, transcendentals=ROWS * count
        ),
        name="attend_last" if last else "attend_block",
    )(query, bias, pos, lengths, *state, *pieces)


def on_device(hidden, w_query, w_key, w_value, prompt_len, page_table):
    g, z, y, c, x = (lax.axis_index(name) for name in ("g", "z", "y", "c", "x"))
    local = hidden[0]

    quarter, w_query, w_key, w_value = together(
        lax.dynamic_slice_in_dim(local, x * 64, 64, 0), w_query, w_key, w_value
    )
    quarter = shift(quarter, "g", 1)

    with jax.named_scope("weights"):
        def head_of(head):
            pieces = [lax.dynamic_slice_in_dim(w, head * HD, HD, 1) for w in (w_key, w_value, w_query)]
            return jnp.concatenate(pieces, axis=1)

        mine = head_of(2 * g + c)
        other, page_table, prompt_len = together(shift(head_of(2 * g + 1 - c), "c", 1), page_table, prompt_len)
        both = jnp.where(c == 0, jnp.concatenate([mine, other]), jnp.concatenate([other, mine]))

    with jax.named_scope("tables"):
        def chips_of(dz, dy):
            return ((z + jnp.array(dz)) % 4) * 4 + (y + jnp.array(dy)) % 4

        first = chips_of([0, 0, 0], [0, 1, 3])
        column, near, back = [chips_of([1, 2, 3], [k, k, k]) for k in (0, 1, 3)]
        opposite = chips_of([0, 1, 2, 3], [2, 2, 2, 2])
        places = jnp.stack([g, c, 1 - c])
        table = jnp.concatenate([first[:1], column, first[1:], near, back, opposite, places]).astype(jnp.int32)
        per_chunk = CHUNK // PAGE
        pad = jnp.full((1,), -1, jnp.int32)
        order = jnp.concatenate([first, pad, column, pad, near, pad, back, pad, opposite]).astype(jnp.int32)
        pages = (order[:, None] * per_chunk + jnp.arange(per_chunk)[None, :]).reshape(-1)
        pos = (pages[:, None] * PAGE + jnp.arange(PAGE)[None, :]).reshape(5, 1, HD * PAGE).astype(jnp.int32)
        chip = z * 4 + y
        row_count = CHUNK // STEPS
        own_table = lax.dynamic_slice_in_dim(page_table, chip * row_count, row_count, 0)
        own_len = lax.dynamic_slice_in_dim(prompt_len, chip * row_count, row_count, 0)
        listed = jnp.any(own_table[:, :, None] == pages[None, None, :], axis=1)
        listed &= pages[None, :] * PAGE < own_len[:, None]
        listed = jnp.repeat(listed, STEPS, axis=0)
        lengths = jnp.repeat(own_len, STEPS)[:, None]
        earlier = jnp.broadcast_to((pages // per_chunk < chip)[None, :], listed.shape)
        bias = jnp.where(jnp.concatenate([earlier, listed]), 0.0, NEG).astype(jnp.bfloat16)

    with jax.named_scope("near_weights"):
        next_1, next_3, quarter, both, local_other = together(
            shift(both, "y", 1), shift(both, "y", 3), quarter, both, shift(local, "c", 1)
        )
        *blocks, quarter_1, quarter_3, table, bias, pos, lengths = together(
            *[shift(both, "z", k) for k in (1, 2, 3)], shift(quarter, "x", 1), shift(quarter, "x", 3),
            table, bias, pos, lengths,
        )
        blocks += [next_1, next_3]

    with jax.named_scope("hidden"):
        sides, (low, high) = side_columns(
            blocks, shift(quarter_1[:32], "x", 1), shift(quarter_3[32:], "x", 3)
        )
        pieces = [both] + blocks + sides + opposite_halves(blocks, sides)
        remote = jnp.zeros_like(local)
        for place, piece in (
            (x, quarter),
            ((x + 1) % 4, quarter_1),
            ((x + 3) % 4, quarter_3),
            ((x + 2) % 4, jnp.concatenate([low, high])),
        ):
            remote = lax.dynamic_update_slice_in_dim(remote, piece, place * 64, 0)
        hiddens = (local, local_other, remote, shift(remote, "c", 1))

    prompt, weights = project_prompt(table, hiddens, pieces)
    fresh, query = project_rest(table, hiddens, weights)

    def attend_parts(k, state, parts):
        keys = sum(part.shape[0] for part in parts)
        return attend_block(
            state, query, bias[:, k * HD:(k + 1) * HD], pos[k, :, :keys], lengths, parts, k == 4
        )

    with jax.named_scope("cache"):
        *blocks, fresh, query = together(*near_blocks(prompt), fresh, query)
        state = attend_own(query, prompt, fresh)
        state = attend_parts(0, state, [prompt, blocks[3], blocks[4]])
        state = attend_parts(1, state, blocks[:3])
        sides, state = side_columns(blocks, *state)
        halves = opposite_halves(blocks, sides)
        state = attend_parts(2, state, sides[:1])
        state = attend_parts(3, state, sides[1:])
        state = attend_parts(4, state, halves)
    out = state

    with jax.named_scope("output"):
        tiles = out.reshape(2, 2, TILE, HD)

        def tile_of(group, core):
            return lax.dynamic_slice(tiles, (group, core, 0, 0), (1, 1, TILE, HD))[0, 0]

        def ordered(first, second, index, along):
            return jnp.where(
                index == 0, jnp.concatenate([first, second], along), jnp.concatenate([second, first], along)
            )

        across = lax.ppermute(tile_of(1 - g, 1 - c), ("g", "c"), [(k, 3 - k) for k in range(4)])
        over = shift(tile_of(1 - g, c), "g", 1)
        beside = shift(tile_of(g, 1 - c), "c", 1)
        result = ordered(ordered(tile_of(g, c), beside, c, 1), ordered(over, across, c, 1), g, 1)
    return result[None]


def solution(mesh):
    names = ("g", "z", "y", "c", "x")
    split = Mesh(mesh.devices.reshape([SIZES[name] for name in names]), names)
    weight = P(("z", "y", "c"), "x")
    return jax.shard_map(
        on_device,
        mesh=split,
        in_specs=(P("g", ("z", "y", "c"), None), weight, weight, weight, P(), P()),
        out_specs=P("g", ("z", "y", "c"), "x"),
        check_vma=False,
    )
```

```python
import functools

import jax
import jax.numpy as jnp
from jax import lax
from jax.experimental import pallas as pl
from jax.experimental.pallas import tpu as pltpu
from jax.sharding import Mesh, PartitionSpec as P

HD = 128
PAGE = 16
STEPS = 4
NEG = -1e30
SCALE = HD ** -0.5 * 1.4426950408889634
SIZES = {"g": 2, "z": 4, "y": 4, "c": 2, "x": 4}
CHUNK = 512
TILE = 256
ROWS = 2 * CHUNK
MIB = 1024 * 1024
VMEM = pl.BlockSpec(memory_space=pltpu.VMEM)


def shift(value, axis, by):
    count = SIZES[axis]
    return lax.ppermute(value, axis, [((k + by) % count, k) for k in range(count)])


def together(*values):
    return lax.optimization_barrier(values)


def second_stage(own, first, *beside):
    pair = jnp.concatenate(first[:2], axis=0)
    *blocks, = together(shift(pair, "y", 1), shift(pair, "y", 3), shift(own, "z", 2), *beside)
    return blocks[:3], blocks[3:]


def third_stage(first, second, *beside):
    half = first[0].shape[0] // 2
    upper = jnp.concatenate([first[2], second[0][:half]], axis=0)
    *blocks, = together(
        shift(second[2], "y", 1), shift(second[2], "y", 3), shift(upper, "y", 1), shift(second[1][half:], "y", 3), *beside
    )
    return blocks[:4], blocks[4:]


def last_stage(third):
    half = third[0].shape[0] // 2
    return [shift(third[0][:half], "y", 1), shift(third[1][half:], "y", 3)]


def dot(left, right):
    return jnp.dot(left, right, preferred_element_type=jnp.float32).astype(jnp.bfloat16)


def project_prompt_kernel(table, *refs):
    pieces, hiddens = refs[:14], refs[14:18]
    kv_out, w_all = refs[18:]
    place = 0
    for piece in pieces:
        for start in range(0, piece.shape[0], 128):
            rows = pl.ds(pl.multiple_of(table[place] * 128, 128), 128)
            w_all[rows, :] = piece[pl.ds(start, 128), :]
            place += 1
    for group in range(2):
        @pl.when(table[32] == group)
        def own_group():
            for k in range(2):
                rows = pl.ds(pl.multiple_of(table[33 + k] * 256, 256), 256)
                kv_out[rows, :] = dot(hiddens[2 * group + k][...], w_all[:, :2 * HD])


def project_rest_kernel(table, w_all, *refs):
    hiddens = refs[:4]
    kv_out, q_out = refs[4:]
    for group in range(2):
        @pl.when(table[32] == group)
        def own_group():
            for k in range(2):
                start = pl.multiple_of(table[33 + k] * 256, 256)
                q_out[pl.ds(start, 256), :] = dot(hiddens[2 * group + k][...], w_all[:, 2 * HD:])
                result = dot(hiddens[2 - 2 * group + k][...], w_all[...])
                kv_out[pl.ds(start, 256), :] = result[:, :2 * HD]
                q_out[pl.ds(CHUNK + start, 256), :] = result[:, 2 * HD:]


def project_prompt(table, hiddens, pieces):
    return pl.pallas_call(
        project_prompt_kernel,
        out_shape=(
            jax.ShapeDtypeStruct((CHUNK, 2 * HD), jnp.bfloat16),
            jax.ShapeDtypeStruct((4096, 3 * HD), jnp.bfloat16),
        ),
        in_specs=[pl.BlockSpec(memory_space=pltpu.SMEM)] + [VMEM] * 18,
        out_specs=(VMEM, VMEM),
        compiler_params=pltpu.CompilerParams(vmem_limit_bytes=8 * MIB),
        cost_estimate=pl.CostEstimate(
            flops=4 * CHUNK * 4096 * 256, bytes_accessed=8 * MIB, transcendentals=0
        ),
        name="project_prompt",
    )(table, *pieces, *hiddens)


def project_rest(table, hiddens, weights):
    return pl.pallas_call(
        project_rest_kernel,
        out_shape=(
            jax.ShapeDtypeStruct((CHUNK, 2 * HD), jnp.bfloat16),
            jax.ShapeDtypeStruct((ROWS, HD), jnp.bfloat16),
        ),
        in_specs=[pl.BlockSpec(memory_space=pltpu.SMEM)] + [VMEM] * 5,
        out_specs=(VMEM, VMEM),
        compiler_params=pltpu.CompilerParams(vmem_limit_bytes=8 * MIB),
        cost_estimate=pl.CostEstimate(
            flops=4 * ROWS * 4096 * 256, bytes_accessed=8 * MIB, transcendentals=0
        ),
        name="project_rest",
    )(table, weights, *hiddens)


def scores_of(query, keys):
    return lax.dot_general(query, keys, (((1,), (1,)), ((), ())), preferred_element_type=jnp.float32)


def attend_own_kernel(q_ref, prompt_ref, fresh_ref, top, acc):
    for tile in range(4):
        rows = pl.ds(tile * TILE, TILE)
        own_ref = prompt_ref if tile < 2 else fresh_ref
        first = 0 if tile < 2 else (tile - 2) * TILE
        count = (tile % 2 + 1) * TILE - first
        query_pos = tile % 2 * TILE - first + lax.broadcasted_iota(jnp.int32, (TILE, count), 0)
        key_pos = lax.broadcasted_iota(jnp.int32, (TILE, count), 1)
        allowed = key_pos <= query_pos
        if tile >= 2:
            allowed &= (key_pos >> 2) == (query_pos >> 2)
        scores = scores_of(q_ref[rows, :], own_ref[pl.ds(first, count), :HD])
        scores = jnp.where(allowed, scores, NEG)
        best = jnp.max(scores, axis=1, keepdims=True)
        weights = jnp.exp2((scores - best) * SCALE).astype(jnp.bfloat16)
        own_vals = jnp.concatenate(
            [own_ref[pl.ds(first, count), HD:], jnp.ones((count, HD), jnp.bfloat16)], axis=1
        )
        acc[rows, :] = jnp.dot(weights, own_vals, preferred_element_type=jnp.float32)
        top[rows, :] = jnp.broadcast_to(best, (TILE, HD))


STATE = (
    jax.ShapeDtypeStruct((ROWS, HD), jnp.float32),
    jax.ShapeDtypeStruct((ROWS, 2 * HD), jnp.float32),
)


def attend_own(query, prompt, fresh):
    return pl.pallas_call(
        attend_own_kernel,
        out_shape=STATE,
        in_specs=[VMEM] * 3,
        out_specs=(VMEM, VMEM),
        compiler_params=pltpu.CompilerParams(vmem_limit_bytes=8 * MIB),
        cost_estimate=pl.CostEstimate(
            flops=4 * ROWS * 512 * 256, bytes_accessed=2 * MIB, transcendentals=ROWS * 384
        ),
        name="attend_own",
    )(query, prompt, fresh)


def attend_block_kernel(count, last, q_ref, bias_ref, pos_ref, len_ref, top_in, acc_in, *rest):
    pieces, rest = rest[:count], rest[count:]
    if last:
        out_ref, keys, vals = rest
    else:
        top_out, acc_out, keys, vals = rest
    block = keys.shape[0]
    row_page = lax.broadcasted_iota(jnp.int32, (block, HD), 0) >> 4
    column = lax.broadcasted_iota(jnp.int32, (block, HD), 1)
    start = 0
    for piece in pieces:
        part = pl.ds(start, piece.shape[0])
        keys[part, :HD] = piece[:, :HD]
        vals[part, :HD] = piece[:, HD:]
        start += piece.shape[0]
    keys[:, HD:] = jnp.where(row_page == column, 1.0, 0.0).astype(jnp.bfloat16)
    vals[:, HD:] = jnp.ones((block, HD), jnp.bfloat16)

    for tile in range(4):
        rows = pl.ds(tile * TILE, TILE)
        query = jnp.concatenate([q_ref[rows, :], bias_ref[rows, :]], axis=1)
        scores = scores_of(query, keys[...])
        if tile >= 2:
            length = len_ref[pl.ds((tile - 2) * TILE, TILE), :]
            scores = jnp.where(pos_ref[...] < length, scores, NEG)
        before = top_in[rows, :1]
        best = jnp.maximum(before, jnp.max(scores, axis=1, keepdims=True))
        weights = jnp.exp2((scores - best) * SCALE).astype(jnp.bfloat16)
        summed = jnp.dot(weights, vals[...], preferred_element_type=jnp.float32)
        state = acc_in[rows, :] * jnp.exp2((before - best) * SCALE) + summed
        if last:
            out_ref[rows, :] = (state[:, :HD] / state[:, HD:]).astype(jnp.bfloat16)
        else:
            acc_out[rows, :] = state
            top_out[rows, :] = jnp.broadcast_to(best, (TILE, HD))


def attend_block(state, query, bias, pos, lengths, pieces, last=False):
    count = sum(piece.shape[0] for piece in pieces)
    return pl.pallas_call(
        functools.partial(attend_block_kernel, len(pieces), last),
        out_shape=jax.ShapeDtypeStruct((ROWS, HD), jnp.bfloat16) if last else STATE,
        in_specs=[VMEM] * (6 + len(pieces)),
        out_specs=VMEM if last else (VMEM, VMEM),
        scratch_shapes=[pltpu.VMEM((count, 2 * HD), jnp.bfloat16)] * 2,
        compiler_params=pltpu.CompilerParams(vmem_limit_bytes=20 * MIB),
        cost_estimate=pl.CostEstimate(
            flops=4 * ROWS * count * 256, bytes_accessed=4 * MIB, transcendentals=ROWS * count
        ),
        name="attend_last" if last else "attend_block",
    )(query, bias, pos, lengths, *state, *pieces)


def on_device(hidden, w_query, w_key, w_value, prompt_len, page_table):
    g, z, y, c, x = (lax.axis_index(name) for name in ("g", "z", "y", "c", "x"))
    local = hidden[0]

    with jax.named_scope("weights"):
        def head_of(head):
            pieces = [lax.dynamic_slice_in_dim(w, head * HD, HD, 1) for w in (w_key, w_value, w_query)]
            return jnp.concatenate(pieces, axis=1)

        quarter = shift(lax.dynamic_slice_in_dim(local, x * 64, 64, 0), "g", 1)
        mine = head_of(2 * g + c)
        other, page_table, prompt_len = together(shift(head_of(2 * g + 1 - c), "c", 1), page_table, prompt_len)
        both = jnp.where(c == 0, jnp.concatenate([mine, other]), jnp.concatenate([other, mine]))

    with jax.named_scope("tables"):
        def chips_of(dz, dy):
            return ((z + jnp.array(dz)) % 4) * 4 + (y + jnp.array(dy)) % 4

        groups = [
            chips_of([0, 1, 3], [0, 0, 0]),
            chips_of([0, 0], [1, 3]),
            chips_of([1, 3, 1, 3], [1, 1, 3, 3]),
            chips_of([2, 2, 2], [0, 1, 3]),
            chips_of([0, 1, 3], [2, 2, 2]),
            chips_of([2], [2]),
        ]
        places = jnp.stack([g, c, 1 - c])
        halves = (jnp.concatenate(groups)[:, None] * 2 + jnp.arange(2)).reshape(-1)
        table = jnp.concatenate([halves, places]).astype(jnp.int32)
        per_chunk = CHUNK // PAGE
        order = jnp.concatenate(
            [jnp.pad(group, (0, 4 - group.shape[0]), constant_values=-1) for group in groups]
        ).astype(jnp.int32)
        pages = (order[:, None] * per_chunk + jnp.arange(per_chunk)[None, :]).reshape(-1)
        pos = (pages[:, None] * PAGE + jnp.arange(PAGE)[None, :]).reshape(6, 1, HD * PAGE).astype(jnp.int32)
        chip = z * 4 + y
        row_count = CHUNK // STEPS
        own_table = lax.dynamic_slice_in_dim(page_table, chip * row_count, row_count, 0)
        own_len = lax.dynamic_slice_in_dim(prompt_len, chip * row_count, row_count, 0)
        listed = jnp.any(own_table[:, :, None] == pages[None, None, :], axis=1)
        listed &= pages[None, :] * PAGE < own_len[:, None]
        listed = jnp.repeat(listed, STEPS, axis=0)
        lengths = jnp.repeat(own_len, STEPS)[:, None]
        earlier = jnp.broadcast_to((pages // per_chunk < chip)[None, :], listed.shape)
        bias = jnp.where(jnp.concatenate([earlier, listed]), 0.0, NEG).astype(jnp.bfloat16)

    with jax.named_scope("near_weights"):
        next_1, next_3, quarter, both, local_other, table, bias, pos, lengths = together(
            shift(both, "y", 1), shift(both, "y", 3), quarter, both, shift(local, "c", 1), table, bias, pos, lengths
        )
        *first, quarter_1, quarter_3, both = together(
            shift(both, "z", 1), shift(both, "z", 3), shift(quarter, "x", 1), shift(quarter, "x", 3), both
        )
        first += [next_1, next_3]

    with jax.named_scope("hidden"):
        second, (low, high) = second_stage(
            both, first, shift(quarter_1[:32], "x", 1), shift(quarter_3[32:], "x", 3)
        )
        third, _ = third_stage(first, second)
        pieces = [both] + first + second + third + last_stage(third)
        remote = jnp.zeros_like(local)
        for place, piece in (
            (x, quarter),
            ((x + 1) % 4, quarter_1),
            ((x + 3) % 4, quarter_3),
            ((x + 2) % 4, jnp.concatenate([low, high])),
        ):
            remote = lax.dynamic_update_slice_in_dim(remote, piece, place * 64, 0)
        hiddens = (local, local_other, remote, shift(remote, "c", 1))

    prompt, weights = project_prompt(table, hiddens, pieces)
    fresh, query = project_rest(table, hiddens, weights)

    def attend_parts(k, state, parts):
        keys = sum(part.shape[0] for part in parts)
        return attend_block(
            state, query, bias[:, k * HD:(k + 1) * HD], pos[k, :, :keys], lengths, parts, k == 5
        )

    with jax.named_scope("cache"):
        *first, fresh, query = together(
            *[shift(prompt, axis, k) for axis in "zy" for k in (1, 3)], fresh, query
        )
        state = attend_own(query, prompt, fresh)
        state = attend_parts(0, state, [prompt] + first[:2])
        state = attend_parts(1, state, first[2:])
        second, state = second_stage(prompt, first, *state)
        state = attend_parts(2, state, second[:2])
        third, state = third_stage(first, second, *state)
        halves = last_stage(third)
        state = attend_parts(3, state, second[2:] + third[:2])
        state = attend_parts(4, state, third[2:])
        state = attend_parts(5, state, halves)
    out = state

    with jax.named_scope("output"):
        tiles = out.reshape(2, 2, TILE, HD)

        def tile_of(group, core):
            return lax.dynamic_slice(tiles, (group, core, 0, 0), (1, 1, TILE, HD))[0, 0]

        def ordered(first, second, index, along):
            return jnp.where(
                index == 0, jnp.concatenate([first, second], along), jnp.concatenate([second, first], along)
            )

        across = lax.ppermute(tile_of(1 - g, 1 - c), ("g", "c"), [(k, 3 - k) for k in range(4)])
        over = shift(tile_of(1 - g, c), "g", 1)
        beside = shift(tile_of(g, 1 - c), "c", 1)
        result = ordered(ordered(tile_of(g, c), beside, c, 1), ordered(over, across, c, 1), g, 1)
    return result[None]


def solution(mesh):
    names = ("g", "z", "y", "c", "x")
    split = Mesh(mesh.devices.reshape([SIZES[name] for name in names]), names)
    weight = P(("z", "y", "c"), "x")
    return jax.shard_map(
        on_device,
        mesh=split,
        in_specs=(P("g", ("z", "y", "c"), None), weight, weight, weight, P(), P()),
        out_specs=P("g", ("z", "y", "c"), "x"),
        check_vma=False,
    )
```

```python
import functools

import jax
import jax.numpy as jnp
from jax import lax
from jax.experimental import pallas as pl
from jax.experimental.pallas import tpu as pltpu
from jax.sharding import Mesh, PartitionSpec as P

HD = 128
PAGE = 16
STEPS = 4
NEG = -1e30
SCALE = HD ** -0.5 * 1.4426950408889634
SIZES = {"g": 2, "z": 4, "y": 4, "c": 2, "x": 4}
CHUNK = 512
TILE = 256
ROWS = 2 * CHUNK
MIB = 1024 * 1024
VMEM = pl.BlockSpec(memory_space=pltpu.VMEM)


def shift(value, axis, by):
    count = SIZES[axis]
    return lax.ppermute(value, axis, [((k + by) % count, k) for k in range(count)])


def together(*values):
    return lax.optimization_barrier(values)


def side_columns(blocks, *beside):
    column = jnp.concatenate(blocks[:3], axis=0)
    near, back, *beside = together(shift(column, "y", 1), shift(column, "y", 3), *beside)
    return [near, back], beside


def opposite_halves(blocks, sides):
    rows = blocks[0].shape[0]
    half_a = shift(jnp.concatenate([blocks[3], sides[0][:rows]], axis=0), "y", 1)
    return [half_a, shift(sides[1][rows:], "y", 3)]


def second_stage(own, first, *beside):
    pair = jnp.concatenate(first[:2], axis=0)
    *blocks, = together(shift(pair, "y", 1), shift(pair, "y", 3), shift(own, "z", 2), *beside)
    return blocks[:3], blocks[3:]


def third_stage(first, second, *beside):
    half = first[0].shape[0] // 2
    upper = jnp.concatenate([first[2], second[0][:half]], axis=0)
    *blocks, = together(
        shift(second[2], "y", 1), shift(second[2], "y", 3), shift(upper, "y", 1), shift(second[1][half:], "y", 3), *beside
    )
    return blocks[:4], blocks[4:]


def last_stage(third):
    half = third[0].shape[0] // 2
    return [shift(third[0][:half], "y", 1), shift(third[1][half:], "y", 3)]


def dot(left, right):
    return jnp.dot(left, right, preferred_element_type=jnp.float32).astype(jnp.bfloat16)


def project_prompt_kernel(table, *refs):
    pieces, hiddens = refs[:10], refs[10:14]
    kv_out, w_all = refs[14:]
    place = 0
    for piece in pieces:
        for start in range(0, piece.shape[0], 256):
            rows = pl.ds(pl.multiple_of(table[place] * 256, 256), 256)
            w_all[rows, :] = piece[pl.ds(start, 256), :]
            place += 1
    for group in range(2):
        @pl.when(table[16] == group)
        def own_group():
            for k in range(2):
                rows = pl.ds(pl.multiple_of(table[17 + k] * 256, 256), 256)
                kv_out[rows, :] = dot(hiddens[2 * group + k][...], w_all[:, :2 * HD])


def project_rest_kernel(table, w_all, *refs):
    hiddens = refs[:4]
    kv_out, q_out = refs[4:]
    for group in range(2):
        @pl.when(table[16] == group)
        def own_group():
            for k in range(2):
                start = pl.multiple_of(table[17 + k] * 256, 256)
                q_out[pl.ds(start, 256), :] = dot(hiddens[2 * group + k][...], w_all[:, 2 * HD:])
                result = dot(hiddens[2 - 2 * group + k][...], w_all[...])
                kv_out[pl.ds(start, 256), :] = result[:, :2 * HD]
                q_out[pl.ds(CHUNK + start, 256), :] = result[:, 2 * HD:]


def project_prompt(table, hiddens, pieces):
    return pl.pallas_call(
        project_prompt_kernel,
        out_shape=(
            jax.ShapeDtypeStruct((CHUNK, 2 * HD), jnp.bfloat16),
            jax.ShapeDtypeStruct((4096, 3 * HD), jnp.bfloat16),
        ),
        in_specs=[pl.BlockSpec(memory_space=pltpu.SMEM)] + [VMEM] * 14,
        out_specs=(VMEM, VMEM),
        compiler_params=pltpu.CompilerParams(vmem_limit_bytes=8 * MIB),
        cost_estimate=pl.CostEstimate(
            flops=4 * CHUNK * 4096 * 256, bytes_accessed=8 * MIB, transcendentals=0
        ),
        name="project_prompt",
    )(table, *pieces, *hiddens)


def project_rest(table, hiddens, weights):
    return pl.pallas_call(
        project_rest_kernel,
        out_shape=(
            jax.ShapeDtypeStruct((CHUNK, 2 * HD), jnp.bfloat16),
            jax.ShapeDtypeStruct((ROWS, HD), jnp.bfloat16),
        ),
        in_specs=[pl.BlockSpec(memory_space=pltpu.SMEM)] + [VMEM] * 5,
        out_specs=(VMEM, VMEM),
        compiler_params=pltpu.CompilerParams(vmem_limit_bytes=8 * MIB),
        cost_estimate=pl.CostEstimate(
            flops=4 * ROWS * 4096 * 256, bytes_accessed=8 * MIB, transcendentals=0
        ),
        name="project_rest",
    )(table, weights, *hiddens)


def scores_of(query, keys):
    return lax.dot_general(query, keys, (((1,), (1,)), ((), ())), preferred_element_type=jnp.float32)


def attend_own_kernel(q_ref, prompt_ref, fresh_ref, top, acc):
    for tile in range(4):
        rows = pl.ds(tile * TILE, TILE)
        own_ref = prompt_ref if tile < 2 else fresh_ref
        first = 0 if tile < 2 else (tile - 2) * TILE
        count = (tile % 2 + 1) * TILE - first
        query_pos = tile % 2 * TILE - first + lax.broadcasted_iota(jnp.int32, (TILE, count), 0)
        key_pos = lax.broadcasted_iota(jnp.int32, (TILE, count), 1)
        allowed = key_pos <= query_pos
        if tile >= 2:
            allowed &= (key_pos >> 2) == (query_pos >> 2)
        scores = scores_of(q_ref[rows, :], own_ref[pl.ds(first, count), :HD])
        scores = jnp.where(allowed, scores, NEG)
        best = jnp.max(scores, axis=1, keepdims=True)
        weights = jnp.exp2((scores - best) * SCALE).astype(jnp.bfloat16)
        own_vals = jnp.concatenate(
            [own_ref[pl.ds(first, count), HD:], jnp.ones((count, HD), jnp.bfloat16)], axis=1
        )
        acc[rows, :] = jnp.dot(weights, own_vals, preferred_element_type=jnp.float32)
        top[rows, :] = jnp.broadcast_to(best, (TILE, HD))


STATE = (
    jax.ShapeDtypeStruct((ROWS, HD), jnp.float32),
    jax.ShapeDtypeStruct((ROWS, 2 * HD), jnp.float32),
)


def attend_own(query, prompt, fresh):
    return pl.pallas_call(
        attend_own_kernel,
        out_shape=STATE,
        in_specs=[VMEM] * 3,
        out_specs=(VMEM, VMEM),
        compiler_params=pltpu.CompilerParams(vmem_limit_bytes=8 * MIB),
        cost_estimate=pl.CostEstimate(
            flops=4 * ROWS * 512 * 256, bytes_accessed=2 * MIB, transcendentals=ROWS * 384
        ),
        name="attend_own",
    )(query, prompt, fresh)


def attend_block_kernel(count, last, q_ref, bias_ref, pos_ref, len_ref, top_in, acc_in, *rest):
    pieces, rest = rest[:count], rest[count:]
    if last:
        out_ref, keys, vals = rest
    else:
        top_out, acc_out, keys, vals = rest
    block = keys.shape[0]
    row_page = lax.broadcasted_iota(jnp.int32, (block, HD), 0) >> 4
    column = lax.broadcasted_iota(jnp.int32, (block, HD), 1)
    start = 0
    for piece in pieces:
        part = pl.ds(start, piece.shape[0])
        keys[part, :HD] = piece[:, :HD]
        vals[part, :HD] = piece[:, HD:]
        start += piece.shape[0]
    keys[:, HD:] = jnp.where(row_page == column, 1.0, 0.0).astype(jnp.bfloat16)
    vals[:, HD:] = jnp.ones((block, HD), jnp.bfloat16)

    for tile in range(4):
        rows = pl.ds(tile * TILE, TILE)
        query = jnp.concatenate([q_ref[rows, :], bias_ref[rows, :]], axis=1)
        scores = scores_of(query, keys[...])
        if tile >= 2:
            length = len_ref[pl.ds((tile - 2) * TILE, TILE), :]
            scores = jnp.where(pos_ref[...] < length, scores, NEG)
        before = top_in[rows, :1]
        best = jnp.maximum(before, jnp.max(scores, axis=1, keepdims=True))
        weights = jnp.exp2((scores - best) * SCALE).astype(jnp.bfloat16)
        summed = jnp.dot(weights, vals[...], preferred_element_type=jnp.float32)
        state = acc_in[rows, :] * jnp.exp2((before - best) * SCALE) + summed
        if last:
            out_ref[rows, :] = (state[:, :HD] / state[:, HD:]).astype(jnp.bfloat16)
        else:
            acc_out[rows, :] = state
            top_out[rows, :] = jnp.broadcast_to(best, (TILE, HD))


def attend_block(state, query, bias, pos, lengths, pieces, last=False):
    count = sum(piece.shape[0] for piece in pieces)
    return pl.pallas_call(
        functools.partial(attend_block_kernel, len(pieces), last),
        out_shape=jax.ShapeDtypeStruct((ROWS, HD), jnp.bfloat16) if last else STATE,
        in_specs=[VMEM] * (6 + len(pieces)),
        out_specs=VMEM if last else (VMEM, VMEM),
        scratch_shapes=[pltpu.VMEM((count, 2 * HD), jnp.bfloat16)] * 2,
        compiler_params=pltpu.CompilerParams(vmem_limit_bytes=20 * MIB),
        cost_estimate=pl.CostEstimate(
            flops=4 * ROWS * count * 256, bytes_accessed=4 * MIB, transcendentals=ROWS * count
        ),
        name="attend_last" if last else "attend_block",
    )(query, bias, pos, lengths, *state, *pieces)


def on_device(hidden, w_query, w_key, w_value, prompt_len, page_table):
    g, z, y, c, x = (lax.axis_index(name) for name in ("g", "z", "y", "c", "x"))
    local = hidden[0]

    with jax.named_scope("weights"):
        def head_of(head):
            pieces = [lax.dynamic_slice_in_dim(w, head * HD, HD, 1) for w in (w_key, w_value, w_query)]
            return jnp.concatenate(pieces, axis=1)

        quarter = shift(lax.dynamic_slice_in_dim(local, x * 64, 64, 0), "g", 1)
        mine = head_of(2 * g + c)
        other, page_table, prompt_len = together(shift(head_of(2 * g + 1 - c), "c", 1), page_table, prompt_len)
        both = jnp.where(c == 0, jnp.concatenate([mine, other]), jnp.concatenate([other, mine]))

    with jax.named_scope("tables"):
        def chips_of(dz, dy):
            return ((z + jnp.array(dz)) % 4) * 4 + (y + jnp.array(dy)) % 4

        groups = [
            chips_of([0, 1, 3], [0, 0, 0]),
            chips_of([0, 0], [1, 3]),
            chips_of([1, 3, 1, 3], [1, 1, 3, 3]),
            chips_of([2, 2, 2], [0, 1, 3]),
            chips_of([0, 1, 3], [2, 2, 2]),
            chips_of([2], [2]),
        ]
        places = jnp.stack([g, c, 1 - c])
        table = jnp.concatenate([
            chips_of([0, 1, 2, 3], [0, 0, 0, 0]), chips_of([0, 0], [1, 3]),
            *[chips_of([1, 2, 3], [k, k, k]) for k in (1, 3)], chips_of([0, 1, 2, 3], [2, 2, 2, 2]), places,
        ]).astype(jnp.int32)
        per_chunk = CHUNK // PAGE
        order = jnp.concatenate(
            [jnp.pad(group, (0, 4 - group.shape[0]), constant_values=-1) for group in groups]
        ).astype(jnp.int32)
        pages = (order[:, None] * per_chunk + jnp.arange(per_chunk)[None, :]).reshape(-1)
        lane = lax.broadcasted_iota(jnp.int32, (6, 1, 4 * CHUNK), 2)
        chunks = order.reshape(6, 1, 4)
        base = sum(jnp.where(lane // CHUNK == k, chunks[:, :, k:k + 1], 0) for k in range(4))
        pos = base * CHUNK + lane % CHUNK
        chip = z * 4 + y
        row_count = CHUNK // STEPS
        own_table = lax.dynamic_slice_in_dim(page_table, chip * row_count, row_count, 0)
        own_len = lax.dynamic_slice_in_dim(prompt_len, chip * row_count, row_count, 0)
        listed = jnp.any(own_table[:, :, None] == pages[None, None, :], axis=1)
        listed &= pages[None, :] * PAGE < own_len[:, None]
    with jax.named_scope("near_weights"):
        next_1, next_3, quarter, both, local_other, table, listed, pages, own_len, pos = together(
            shift(both, "y", 1), shift(both, "y", 3), quarter, both, shift(local, "c", 1),
            table, listed, pages, own_len, pos,
        )
        *blocks, quarter_1, quarter_3, listed = together(
            *[shift(both, "z", k) for k in (1, 2, 3)], shift(quarter, "x", 1), shift(quarter, "x", 3), listed
        )
        blocks += [next_1, next_3]

    with jax.named_scope("tables"):
        listed = jnp.repeat(listed, STEPS, axis=0)
        lengths = jnp.repeat(own_len, STEPS)[:, None]
        earlier = jnp.broadcast_to((pages // per_chunk < chip)[None, :], listed.shape)
        bias = jnp.where(jnp.concatenate([earlier, listed]), 0.0, NEG).astype(jnp.bfloat16)

    with jax.named_scope("hidden"):
        sides, (low, high, bias, lengths) = side_columns(
            blocks, shift(quarter_1[:32], "x", 1), shift(quarter_3[32:], "x", 3), bias, lengths
        )
        pieces = [both] + blocks + sides + opposite_halves(blocks, sides)
        remote = jnp.zeros_like(local)
        for place, piece in (
            (x, quarter),
            ((x + 1) % 4, quarter_1),
            ((x + 3) % 4, quarter_3),
            ((x + 2) % 4, jnp.concatenate([low, high])),
        ):
            remote = lax.dynamic_update_slice_in_dim(remote, piece, place * 64, 0)
        hiddens = (local, local_other, remote, shift(remote, "c", 1))

    prompt, weights = project_prompt(table, hiddens, pieces)
    fresh, query = project_rest(table, hiddens, weights)

    def attend_parts(k, state, parts):
        keys = sum(part.shape[0] for part in parts)
        return attend_block(
            state, query, bias[:, k * HD:(k + 1) * HD], pos[k, :, :keys], lengths, parts, k == 5
        )

    with jax.named_scope("cache"):
        *first, fresh, query = together(
            *[shift(prompt, axis, k) for axis in "zy" for k in (1, 3)], fresh, query
        )
        state = attend_own(query, prompt, fresh)
        state = attend_parts(0, state, [prompt] + first[:2])
        state = attend_parts(1, state, first[2:])
        second, state = second_stage(prompt, first, *state)
        state = attend_parts(2, state, second[:2])
        third, state = third_stage(first, second, *state)
        halves = last_stage(third)
        state = attend_parts(3, state, second[2:] + third[:2])
        state = attend_parts(4, state, third[2:])
        state = attend_parts(5, state, halves)
    out = state

    with jax.named_scope("output"):
        tiles = out.reshape(2, 2, TILE, HD)

        def tile_of(group, core):
            return lax.dynamic_slice(tiles, (group, core, 0, 0), (1, 1, TILE, HD))[0, 0]

        def ordered(first, second, index, along):
            return jnp.where(
                index == 0, jnp.concatenate([first, second], along), jnp.concatenate([second, first], along)
            )

        across = lax.ppermute(tile_of(1 - g, 1 - c), ("g", "c"), [(k, 3 - k) for k in range(4)])
        over = shift(tile_of(1 - g, c), "g", 1)
        beside = shift(tile_of(g, 1 - c), "c", 1)
        result = ordered(ordered(tile_of(g, c), beside, c, 1), ordered(over, across, c, 1), g, 1)
    return result[None]


def solution(mesh):
    names = ("g", "z", "y", "c", "x")
    split = Mesh(mesh.devices.reshape([SIZES[name] for name in names]), names)
    weight = P(("z", "y", "c"), "x")
    return jax.shard_map(
        on_device,
        mesh=split,
        in_specs=(P("g", ("z", "y", "c"), None), weight, weight, weight, P(), P()),
        out_specs=P("g", ("z", "y", "c"), "x"),
        check_vma=False,
    )
```

```python
import functools

import jax
import jax.numpy as jnp
from jax import lax
from jax.experimental import pallas as pl
from jax.experimental.pallas import tpu as pltpu
from jax.sharding import Mesh, PartitionSpec as P

HD = 128
PAGE = 16
STEPS = 4
NEG = -1e30
SCALE = HD ** -0.5 * 1.4426950408889634
SIZES = {"g": 2, "z": 4, "y": 4, "c": 2, "x": 4}
CHUNK = 512
TILE = 256
ROWS = 2 * CHUNK
MIB = 1024 * 1024
VMEM = pl.BlockSpec(memory_space=pltpu.VMEM)


def shift(value, axis, by):
    count = SIZES[axis]
    return lax.ppermute(value, axis, [((k + by) % count, k) for k in range(count)])


def together(*values):
    return lax.optimization_barrier(values)


def near_blocks(value):
    return [shift(value, "z", k) for k in (1, 2, 3)] + [shift(value, "y", k) for k in (1, 3)]


def side_columns(blocks, *beside):
    column = jnp.concatenate(blocks[:3], axis=0)
    near, back, *beside = together(shift(column, "y", 1), shift(column, "y", 3), *beside)
    return [near, back], beside


def opposite_halves(blocks, sides):
    rows = blocks[0].shape[0]
    half_a = shift(jnp.concatenate([blocks[3], sides[0][:rows]], axis=0), "y", 1)
    return [half_a, shift(sides[1][rows:], "y", 3)]


def dot(left, right):
    return jnp.dot(left, right, preferred_element_type=jnp.float32).astype(jnp.bfloat16)


def project_prompt_kernel(table, *refs):
    pieces, hiddens = refs[:10], refs[10:14]
    kv_out, w_all = refs[14:]
    place = 0
    for piece in pieces:
        for start in range(0, piece.shape[0], 256):
            rows = pl.ds(pl.multiple_of(table[place] * 256, 256), 256)
            w_all[rows, :] = piece[pl.ds(start, 256), :]
            place += 1
    for group in range(2):
        @pl.when(table[16] == group)
        def own_group():
            for k in range(2):
                rows = pl.ds(pl.multiple_of(table[17 + k] * 256, 256), 256)
                kv_out[rows, :] = dot(hiddens[2 * group + k][...], w_all[:, :2 * HD])


def project_rest_kernel(table, w_all, *refs):
    hiddens = refs[:4]
    kv_out, q_out = refs[4:]
    for group in range(2):
        @pl.when(table[16] == group)
        def own_group():
            for k in range(2):
                start = pl.multiple_of(table[17 + k] * 256, 256)
                q_out[pl.ds(start, 256), :] = dot(hiddens[2 * group + k][...], w_all[:, 2 * HD:])
                result = dot(hiddens[2 - 2 * group + k][...], w_all[...])
                kv_out[pl.ds(start, 256), :] = result[:, :2 * HD]
                q_out[pl.ds(CHUNK + start, 256), :] = result[:, 2 * HD:]


def project_prompt(table, hiddens, pieces):
    return pl.pallas_call(
        project_prompt_kernel,
        out_shape=(
            jax.ShapeDtypeStruct((CHUNK, 2 * HD), jnp.bfloat16),
            jax.ShapeDtypeStruct((4096, 3 * HD), jnp.bfloat16),
        ),
        in_specs=[pl.BlockSpec(memory_space=pltpu.SMEM)] + [VMEM] * 14,
        out_specs=(VMEM, VMEM),
        compiler_params=pltpu.CompilerParams(vmem_limit_bytes=8 * MIB),
        cost_estimate=pl.CostEstimate(
            flops=4 * CHUNK * 4096 * 256, bytes_accessed=8 * MIB, transcendentals=0
        ),
        name="project_prompt",
    )(table, *pieces, *hiddens)


def project_rest(table, hiddens, weights):
    return pl.pallas_call(
        project_rest_kernel,
        out_shape=(
            jax.ShapeDtypeStruct((CHUNK, 2 * HD), jnp.bfloat16),
            jax.ShapeDtypeStruct((ROWS, HD), jnp.bfloat16),
        ),
        in_specs=[pl.BlockSpec(memory_space=pltpu.SMEM)] + [VMEM] * 5,
        out_specs=(VMEM, VMEM),
        compiler_params=pltpu.CompilerParams(vmem_limit_bytes=8 * MIB),
        cost_estimate=pl.CostEstimate(
            flops=4 * ROWS * 4096 * 256, bytes_accessed=8 * MIB, transcendentals=0
        ),
        name="project_rest",
    )(table, weights, *hiddens)


def scores_of(query, keys):
    return lax.dot_general(query, keys, (((1,), (1,)), ((), ())), preferred_element_type=jnp.float32)


def attend_own_kernel(q_ref, prompt_ref, fresh_ref, top, acc):
    for tile in range(4):
        rows = pl.ds(tile * TILE, TILE)
        own_ref = prompt_ref if tile < 2 else fresh_ref
        first = 0 if tile < 2 else (tile - 2) * TILE
        count = (tile % 2 + 1) * TILE - first
        query_pos = tile % 2 * TILE - first + lax.broadcasted_iota(jnp.int32, (TILE, count), 0)
        key_pos = lax.broadcasted_iota(jnp.int32, (TILE, count), 1)
        allowed = key_pos <= query_pos
        if tile >= 2:
            allowed &= (key_pos >> 2) == (query_pos >> 2)
        scores = scores_of(q_ref[rows, :], own_ref[pl.ds(first, count), :HD])
        scores = jnp.where(allowed, scores, NEG)
        best = jnp.max(scores, axis=1, keepdims=True)
        weights = jnp.exp2((scores - best) * SCALE).astype(jnp.bfloat16)
        own_vals = jnp.concatenate(
            [own_ref[pl.ds(first, count), HD:], jnp.ones((count, HD), jnp.bfloat16)], axis=1
        )
        acc[rows, :] = jnp.dot(weights, own_vals, preferred_element_type=jnp.float32)
        top[rows, :] = jnp.broadcast_to(best, (TILE, HD))


STATE = (
    jax.ShapeDtypeStruct((ROWS, HD), jnp.float32),
    jax.ShapeDtypeStruct((ROWS, 2 * HD), jnp.float32),
)


def attend_own(query, prompt, fresh):
    return pl.pallas_call(
        attend_own_kernel,
        out_shape=STATE,
        in_specs=[VMEM] * 3,
        out_specs=(VMEM, VMEM),
        compiler_params=pltpu.CompilerParams(vmem_limit_bytes=8 * MIB),
        cost_estimate=pl.CostEstimate(
            flops=4 * ROWS * 512 * 256, bytes_accessed=2 * MIB, transcendentals=ROWS * 384
        ),
        name="attend_own",
    )(query, prompt, fresh)


def attend_block_kernel(count, last, q_ref, bias_ref, pos_ref, len_ref, top_in, acc_in, *rest):
    pieces, rest = rest[:count], rest[count:]
    if last:
        out_ref, keys, vals = rest
    else:
        top_out, acc_out, keys, vals = rest
    block = keys.shape[0]
    row_page = lax.broadcasted_iota(jnp.int32, (block, HD), 0) >> 4
    column = lax.broadcasted_iota(jnp.int32, (block, HD), 1)
    start = 0
    for piece in pieces:
        part = pl.ds(start, piece.shape[0])
        keys[part, :HD] = piece[:, :HD]
        vals[part, :HD] = piece[:, HD:]
        start += piece.shape[0]
    keys[:, HD:] = jnp.where(row_page == column, 1.0, 0.0).astype(jnp.bfloat16)
    vals[:, HD:] = jnp.ones((block, HD), jnp.bfloat16)

    for tile in range(4):
        rows = pl.ds(tile * TILE, TILE)
        query = jnp.concatenate([q_ref[rows, :], bias_ref[rows, :]], axis=1)
        scores = scores_of(query, keys[...])
        if tile >= 2:
            length = len_ref[pl.ds((tile - 2) * TILE, TILE), :]
            scores = jnp.where(pos_ref[...] < length, scores, NEG)
        before = top_in[rows, :1]
        best = jnp.maximum(before, jnp.max(scores, axis=1, keepdims=True))
        weights = jnp.exp2((scores - best) * SCALE).astype(jnp.bfloat16)
        summed = jnp.dot(weights, vals[...], preferred_element_type=jnp.float32)
        state = acc_in[rows, :] * jnp.exp2((before - best) * SCALE) + summed
        if last:
            out_ref[rows, :] = (state[:, :HD] / state[:, HD:]).astype(jnp.bfloat16)
        else:
            acc_out[rows, :] = state
            top_out[rows, :] = jnp.broadcast_to(best, (TILE, HD))


def attend_block(state, query, bias, pos, lengths, pieces, last=False):
    count = sum(piece.shape[0] for piece in pieces)
    return pl.pallas_call(
        functools.partial(attend_block_kernel, len(pieces), last),
        out_shape=jax.ShapeDtypeStruct((ROWS, HD), jnp.bfloat16) if last else STATE,
        in_specs=[VMEM] * (6 + len(pieces)),
        out_specs=VMEM if last else (VMEM, VMEM),
        scratch_shapes=[pltpu.VMEM((count, 2 * HD), jnp.bfloat16)] * 2,
        compiler_params=pltpu.CompilerParams(vmem_limit_bytes=20 * MIB),
        cost_estimate=pl.CostEstimate(
            flops=4 * ROWS * count * 256, bytes_accessed=4 * MIB, transcendentals=ROWS * count
        ),
        name="attend_last" if last else "attend_block",
    )(query, bias, pos, lengths, *state, *pieces)


def on_device(hidden, w_query, w_key, w_value, prompt_len, page_table):
    g, z, y, c, x = (lax.axis_index(name) for name in ("g", "z", "y", "c", "x"))
    local = hidden[0]

    with jax.named_scope("weights"):
        def head_of(head):
            pieces = [lax.dynamic_slice_in_dim(w, head * HD, HD, 1) for w in (w_key, w_value, w_query)]
            return jnp.concatenate(pieces, axis=1)

        quarter = shift(lax.dynamic_slice_in_dim(local, x * 64, 64, 0), "g", 1)
        mine = head_of(2 * g + c)
        other, page_table, prompt_len = together(shift(head_of(2 * g + 1 - c), "c", 1), page_table, prompt_len)
        both = jnp.where(c == 0, jnp.concatenate([mine, other]), jnp.concatenate([other, mine]))

    with jax.named_scope("tables"):
        def chips_of(dz, dy):
            return ((z + jnp.array(dz)) % 4) * 4 + (y + jnp.array(dy)) % 4

        first = chips_of([0, 0, 0], [0, 1, 3])
        column, near, back = [chips_of([1, 2, 3], [k, k, k]) for k in (0, 1, 3)]
        opposite = chips_of([0, 1, 2, 3], [2, 2, 2, 2])
        places = jnp.stack([g, c, 1 - c])
        table = jnp.concatenate([first[:1], column, first[1:], near, back, opposite, places]).astype(jnp.int32)
        per_chunk = CHUNK // PAGE
        pad = jnp.full((1,), -1, jnp.int32)
        order = jnp.concatenate([first, pad, column, pad, near, pad, back, pad, opposite]).astype(jnp.int32)
        pages = (order[:, None] * per_chunk + jnp.arange(per_chunk)[None, :]).reshape(-1)
        pos = (pages[:, None] * PAGE + jnp.arange(PAGE)[None, :]).reshape(5, 1, HD * PAGE).astype(jnp.int32)
        chip = z * 4 + y
        row_count = CHUNK // STEPS
        own_table = lax.dynamic_slice_in_dim(page_table, chip * row_count, row_count, 0)
        own_len = lax.dynamic_slice_in_dim(prompt_len, chip * row_count, row_count, 0)
        listed = jnp.any(own_table[:, :, None] == pages[None, None, :], axis=1)
        listed &= pages[None, :] * PAGE < own_len[:, None]
        listed = jnp.repeat(listed, STEPS, axis=0)
        lengths = jnp.repeat(own_len, STEPS)[:, None]
        earlier = jnp.broadcast_to((pages // per_chunk < chip)[None, :], listed.shape)
        bias = jnp.where(jnp.concatenate([earlier, listed]), 0.0, NEG).astype(jnp.bfloat16)

    with jax.named_scope("near_weights"):
        next_1, next_3, quarter, both, local_other, table, bias, pos, lengths = together(
            shift(both, "y", 1), shift(both, "y", 3), quarter, both, shift(local, "c", 1), table, bias, pos, lengths
        )
        *blocks, quarter_1, quarter_3 = together(
            *[shift(both, "z", k) for k in (1, 2, 3)], shift(quarter, "x", 1), shift(quarter, "x", 3)
        )
        blocks += [next_1, next_3]

    with jax.named_scope("hidden"):
        sides, (low, high) = side_columns(
            blocks, shift(quarter_1[:32], "x", 1), shift(quarter_3[32:], "x", 3)
        )
        pieces = [both] + blocks + sides + opposite_halves(blocks, sides)
        remote = jnp.zeros_like(local)
        for place, piece in (
            (x, quarter),
            ((x + 1) % 4, quarter_1),
            ((x + 3) % 4, quarter_3),
            ((x + 2) % 4, jnp.concatenate([low, high])),
        ):
            remote = lax.dynamic_update_slice_in_dim(remote, piece, place * 64, 0)
        hiddens = (local, local_other, remote, shift(remote, "c", 1))

    prompt, weights = project_prompt(table, hiddens, pieces)
    fresh, query = project_rest(table, hiddens, weights)

    def attend_parts(k, state, parts):
        keys = sum(part.shape[0] for part in parts)
        return attend_block(
            state, query, bias[:, k * HD:(k + 1) * HD], pos[k, :, :keys], lengths, parts, k == 4
        )

    with jax.named_scope("cache"):
        *blocks, fresh, query = together(*near_blocks(prompt), fresh, query)
        state = attend_own(query, prompt, fresh)
        state = attend_parts(0, state, [prompt, blocks[3], blocks[4]])
        state = attend_parts(1, state, blocks[:3])
        sides, state = side_columns(blocks, *state)
        halves = opposite_halves(blocks, sides)
        state = attend_parts(2, state, sides[:1])
        state = attend_parts(3, state, sides[1:])
        state = attend_parts(4, state, halves)
    out = state

    with jax.named_scope("output"):
        tiles = out.reshape(2, 2, TILE, HD)

        def tile_of(group, core):
            return lax.dynamic_slice(tiles, (group, core, 0, 0), (1, 1, TILE, HD))[0, 0]

        def ordered(first, second, index, along):
            return jnp.where(
                index == 0, jnp.concatenate([first, second], along), jnp.concatenate([second, first], along)
            )

        across = lax.ppermute(tile_of(1 - g, 1 - c), ("g", "c"), [(k, 3 - k) for k in range(4)])
        over = shift(tile_of(1 - g, c), "g", 1)
        beside = shift(tile_of(g, 1 - c), "c", 1)
        result = ordered(ordered(tile_of(g, c), beside, c, 1), ordered(over, across, c, 1), g, 1)
    return result[None]


def solution(mesh):
    names = ("g", "z", "y", "c", "x")
    split = Mesh(mesh.devices.reshape([SIZES[name] for name in names]), names)
    weight = P(("z", "y", "c"), "x")
    return jax.shard_map(
        on_device,
        mesh=split,
        in_specs=(P("g", ("z", "y", "c"), None), weight, weight, weight, P(), P()),
        out_specs=P("g", ("z", "y", "c"), "x"),
        check_vma=False,
    )
```
